32 devices in a mesh: fsdp: 16 (over z, x, core), rep: 2 (over y).
Axes of the slice: x: 2, y: 2, z: 4, core: 2. Of those that a mesh axis runs over, the one named last changes fastest.
Arguments:
- tokens: bfloat16 [8192, 1024], P(('fsdp', 'rep')), may hold values from -6 to 6
- counts: int32 [32], P(('fsdp', 'rep')), may hold values from 128 to 256, as said below
- segments: int32 [8192], P(('fsdp', 'rep')), may hold values from 0 to 8191, as said below
- norm1_gain: bfloat16 [1024], P(('fsdp', 'rep')), may hold values from 0.25 to 1.75
- in_weight: bfloat16 [1024, 3072], P(('fsdp', 'rep')), may hold values from -0.1875 to 0.1875
- conv_kernel: bfloat16 [3, 1024], P(None, ('fsdp', 'rep')), may hold values from -3 to 3
- out_weight: bfloat16 [1024, 1024], P(('fsdp', 'rep')), may hold values from -0.1875 to 0.1875
- norm2_gain: bfloat16 [1024], P(('fsdp', 'rep')), may hold values from 0.25 to 1.75
- gate_weight: bfloat16 [1024, 4608], P(('fsdp', 'rep')), may hold values from -0.1875 to 0.1875
- up_weight: bfloat16 [1024, 4608], P(('fsdp', 'rep')), may hold values from -0.1875 to 0.1875
- down_weight: bfloat16 [4608, 1024], P(('fsdp', 'rep')), may hold values from -0.125 to 0.125
- cotangent: bfloat16 [8192, 1024], P(('fsdp', 'rep')), may hold values from -6 to 6
Outputs:
- mixed: bfloat16 [8192, 1024], P(('fsdp', 'rep'))
- token_grad: float32 [8192, 1024], P(('fsdp', 'rep'))
- norm1_gain_grad: float32 [1024], P(('fsdp', 'rep'))
- in_weight_grad: float32 [1024, 3072], P(('fsdp', 'rep'))
- conv_kernel_grad: float32 [3, 1024], P(None, ('fsdp', 'rep'))
- out_weight_grad: float32 [1024, 1024], P(('fsdp', 'rep'))
- norm2_gain_grad: float32 [1024], P(('fsdp', 'rep'))
- gate_weight_grad: float32 [1024, 4608], P(('fsdp', 'rep'))
- up_weight_grad: float32 [1024, 4608], P(('fsdp', 'rep'))
- down_weight_grad: float32 [4608, 1024], P(('fsdp', 'rep'))
The draws below stay inside these ranges and needn't reach their ends.
Inputs may be any that keep to these rules, and one draw needn't show every extreme that they name: counts[d] is the number of live slots at the front of device block d of 256 rows; some device has all 256 live. `segments`: a sequence's id is the index of its first token slot; ids never fall, and a sequence lies within one aligned block of 256 rows.
All inputs are finite; a program needn't handle non-finite values.
Results may differ from the reference program's by a relative error of at most 0.0097.
Values may be sent and summed in bfloat16 or wider, within the bound.
No kernel may reach another device: no remote copies, remote signals or barrier semaphores. Data moves between devices by JAX's collectives and lax.ppermute only.
A program may use at most 256 MiB of HBM per device.

```python
import jax
import jax.numpy as jnp
from jax import lax

D = 1024
FF = 4608
KW = 3
TOK_DEV = 256
TOKENS = 8192


def draw_counts(key, part):
    key = jax.random.fold_in(key, 11)
    first, second = jax.random.split(key)
    number = TOKENS // TOK_DEV
    drawn = jax.random.randint(first, (number,), TOK_DEV // 2, TOK_DEV + 1)
    full = jax.random.randint(second, (), 0, number)
    return jnp.where(jnp.arange(number) == full, TOK_DEV, drawn).astype(jnp.int32)


def draw_segments(key, part):
    key = jax.random.fold_in(key, 23)
    number = TOKENS // TOK_DEV
    period = max(4, TOK_DEV // 4)
    marks = jax.random.randint(key, (number, TOK_DEV), 0, period) == 0
    marks = marks.at[:, 0].set(True)
    marks = marks.at[number - 1, TOK_DEV - 1].set(True)
    places = jnp.broadcast_to(jnp.arange(TOK_DEV, dtype=jnp.int32)[None, :], (number, TOK_DEV))
    starts = lax.cummax(jnp.where(marks, places, 0), axis=1)
    ids = starts + jnp.arange(number, dtype=jnp.int32)[:, None] * TOK_DEV
    return ids.reshape(-1).astype(jnp.int32)


def level_of(rng, shape, pieces, least, top_value):
    gain = 1.0
    for dim, shards_of in pieces:
        steps = jax.random.uniform(jax.random.fold_in(jax.random.fold_in(rng, 6), dim), (shards_of,), jnp.float32, least / len(pieces), top_value / len(pieces))
        gain = gain * jnp.repeat(jnp.exp(steps), shape[dim] // shards_of).reshape((-1,) + (1,) * (len(shape) - 1 - dim))
    return gain


def noise(rng, extent, deviation, bound, shards=(), kind=jnp.bfloat16):
    values = deviation * jax.random.normal(rng, extent, jnp.float32)
    if shards:
        values = values * level_of(rng, extent, shards, -0.22, 0.18)
    return jnp.clip(values, -bound, bound).astype(kind)


def setup_inputs(seed: int = 0) -> dict:
    splits = jax.random.split(jax.random.key(seed), 13)
    return {
        "tokens": noise(splits[0], (TOKENS, D), 1.0, 6.0, ((0, 32),)),
        "counts": draw_counts(jax.random.fold_in(splits[12], 71), 0),
        "segments": draw_segments(jax.random.fold_in(splits[12], 71), 0),
        "norm1_gain": jnp.clip(1.0 + 0.15 * jax.random.normal(splits[3], (D,), jnp.float32), 0.25, 1.75).astype(jnp.bfloat16),
        "in_weight": noise(splits[4], (D, 3 * D), D ** -0.5, 0.1875, ((0, 32),)),
        "conv_kernel": noise(splits[5], (KW, D), 0.6, 3.0, ((1, 32),)),
        "out_weight": noise(splits[6], (D, D), D ** -0.5, 0.1875, ((0, 32),)),
        "norm2_gain": jnp.clip(1.0 + 0.15 * jax.random.normal(splits[7], (D,), jnp.float32), 0.25, 1.75).astype(jnp.bfloat16),
        "gate_weight": noise(splits[8], (D, FF), D ** -0.5, 0.1875, ((0, 32),)),
        "up_weight": noise(splits[9], (D, FF), D ** -0.5, 0.1875, ((0, 32),)),
        "down_weight": noise(splits[10], (FF, D), (FF // 2) ** -0.5, 0.125, ((0, 32),)),
        "cotangent": noise(splits[11], (TOKENS, D), 1.0, 6.0, ((0, 32),)),
    }


EPS = 1e-05

@jax.custom_vjp
def low(v):
    return lax.optimization_barrier(v.astype(jnp.bfloat16)).astype(jnp.float32)

@jax.custom_vjp
def low_back(v):
    return v

def low_keep(v):
    return (low(v), None)

def low_pass(kept, grad):
    return (grad,)

def back_keep(v):
    return (v, None)

def back_low(kept, grad):
    return (low(grad),)
low.defvjp(low_keep, low_pass)
low_back.defvjp(back_keep, back_low)

def matmul(left, right):
    return jnp.dot(left, right, precision=lax.Precision.HIGHEST, preferred_element_type=jnp.float32)

def shifted(values, steps):
    return jnp.concatenate([jnp.zeros((steps, values.shape[1]), values.dtype), values[:-steps]], axis=0)

def layer(source, seg, count, params):
    gain_one, in_matrix, kernel, out_matrix, gain_two, gate_matrix, up_matrix, down_matrix = params
    width = source.shape[1]
    scale_one = lax.rsqrt(lax.optimization_barrier(jnp.mean(source * source, axis=1, keepdims=True)) + EPS)
    normed_one = low(source * scale_one * gain_one)
    projected = low_back(matmul(normed_one, in_matrix))
    first = projected[:, :width]
    second = projected[:, width:2 * width]
    stream = projected[:, 2 * width:]
    product = first * stream
    same_one = jnp.concatenate([jnp.zeros((1,), source.dtype), (seg[1:] == seg[:-1]).astype(source.dtype)])[:, None]
    same_two = jnp.concatenate([jnp.zeros((2,), source.dtype), (seg[2:] == seg[:-2]).astype(source.dtype)])[:, None]
    convolved = kernel[0] * product + kernel[1] * shifted(product, 1) * same_one + kernel[2] * shifted(product, 2) * same_two
    mixer = low(second * convolved)
    branch = low_back(matmul(mixer, out_matrix))
    hidden = source + branch
    scale_two = lax.rsqrt(lax.optimization_barrier(jnp.mean(hidden * hidden, axis=1, keepdims=True)) + EPS)
    normed_two = low(hidden * scale_two * gain_two)
    gate = low_back(matmul(normed_two, gate_matrix))
    up = low_back(matmul(normed_two, up_matrix))
    act = low(jax.nn.silu(gate) * up)
    ffn = low_back(matmul(act, down_matrix))
    live = (jnp.arange(source.shape[0]) < count).astype(source.dtype)[:, None]
    return live * (hidden + ffn)

def reference(tokens, counts, segments, norm1_gain, in_weight, conv_kernel, out_weight, norm2_gain, gate_weight, up_weight, down_weight, cotangent):
    blocks = TOKENS // TOK_DEV
    params = tuple((w.astype(jnp.float32) for w in (norm1_gain, in_weight, conv_kernel, out_weight, norm2_gain, gate_weight, up_weight, down_weight)))
    source = tokens.astype(jnp.float32).reshape(blocks, TOK_DEV, D)
    seg = segments.reshape(blocks, TOK_DEV)

    def forward(inputs, weights):

        def run(item):
            return layer(item[0], item[1], item[2], weights)
        return lax.map(jax.checkpoint(run), (inputs, seg, counts))
    result, pullback = jax.vjp(forward, source, params)
    grad_in, grad_params = pullback(cotangent.astype(jnp.float32).reshape(blocks, TOK_DEV, D))
    mixed = result.reshape(TOKENS, D).astype(jnp.bfloat16)
    return (mixed, grad_in.reshape(TOKENS, D), grad_params[0], grad_params[1], grad_params[2], grad_params[3], grad_params[4], grad_params[5], grad_params[6], grad_params[7])
```

```python
import jax
import jax.numpy as jnp
from jax import lax
from jax.sharding import Mesh, PartitionSpec as P

EPS = 1e-05
BF = jnp.bfloat16
F32 = jnp.float32

PLANE = ("b", "y")
COLUMN = ("t", "c")
LANES = 256


def rows_by_rows(left, right):
    return lax.dot_general(left, right, (((0,), (0,)), ((), ())), preferred_element_type=F32)


def cols_by_cols(left, right):
    return lax.dot_general(left, right, (((1,), (1,)), ((), ())), preferred_element_type=F32)


def to_peer(values, k):
    return lax.ppermute(values, PLANE, [(i, i ^ k) for i in range(4)])


def plane_gather(values):
    return [values] + [to_peer(values, k) for k in (1, 2, 3)]


def plane_sum(blocks):
    sent = [blocks[k].astype(BF) for k in (1, 2, 3)]
    total = blocks[0].astype(F32)
    for k in (1, 2, 3):
        total = total + to_peer(sent[k - 1], k).astype(F32)
    return total


def pick(blocks, i):
    return lax.dynamic_index_in_dim(blocks, i, 0, keepdims=False)


def plane_swap(blocks, member):
    got = [pick(blocks, member)] + [to_peer(pick(blocks, member ^ k), k) for k in (1, 2, 3)]
    got = jnp.stack(got)
    return jnp.stack([pick(got, member ^ j) for j in range(4)])


def norm_back(grad_norm, source, scale, gain):
    weighted = grad_norm * gain
    gain_grad = jnp.sum(grad_norm * source * scale, axis=0)
    source_grad = scale * weighted - source * scale**3 * jnp.mean(
        weighted * source, axis=1, keepdims=True
    )
    return (source_grad, gain_grad)


def shifted(values, steps):
    return jnp.pad(values, ((0, 0), (steps, 0), (0, 0)))[:, :-steps]


def lifted(values, steps):
    return jnp.pad(values, ((0, 0), (0, steps), (0, 0)))[:, steps:]


def make_local(t):
    nb = 2 * t

    def local(
        tokens,
        counts,
        segments,
        norm1_gain,
        in_weight,
        conv_kernel,
        out_weight,
        norm2_gain,
        gate_weight,
        up_weight,
        down_weight,
        cotangent,
    ):
        slots, width = tokens.shape
        r = in_weight.shape[0]
        ch = out_weight.shape[0]
        h = down_weight.shape[0]
        share = nb * ch
        taps = conv_kernel.shape[0]
        slabs = width // LANES
        member = 2 * lax.axis_index("b") + lax.axis_index("y")

        same_one = jnp.concatenate([jnp.zeros((1,), BF), (segments[1:] == segments[:-1]).astype(BF)])
        same_two = jnp.concatenate([jnp.zeros((2,), BF), (segments[2:] == segments[:-2]).astype(BF)])
        flags = jnp.concatenate([same_one, same_two])
        flags = jnp.pad(flags, (0, 16 * width - 2 * slots)).reshape(16, width)
        live = (jnp.arange(slots) < counts[0]).astype(F32)[:, None]
        dout = cotangent.astype(F32) * live
        dffn_own = dout.astype(BF)

        in_blocks = in_weight.reshape(r, 3, t, 2, 2, 2, ch).transpose(3, 5, 1, 0, 2, 4, 6)
        in_blocks = in_blocks.reshape(4, 3 * r, share)
        extra = jnp.concatenate([norm1_gain, norm2_gain, conv_kernel.reshape(-1)])
        extra = jnp.pad(extra, (0, 16 * share - extra.shape[0])).reshape(1, 16, share)
        conv_blocks = jnp.concatenate([in_blocks, jnp.broadcast_to(extra, (4, 16, share))], axis=1)
        conv_mine = plane_swap(conv_blocks, member)
        out_slabs = out_weight.reshape(ch, slabs, LANES).transpose(1, 0, 2).reshape(slabs * ch, LANES)
        conv_all = lax.all_gather(
            jnp.concatenate([conv_mine.reshape(4 * (3 * r + 16), share), out_slabs]), COLUMN
        )
        gathered = plane_gather(jnp.concatenate([tokens, flags]))
        source = jnp.stack([g[:slots] for g in gathered]).reshape(4 * slots, width).astype(F32)
        marks = jnp.stack([g[slots:].reshape(-1)[: 2 * slots] for g in gathered]).astype(F32)
        same_one = marks[:, :slots, None]
        same_two = marks[:, slots:, None]
        source, same_one, same_two = lax.optimization_barrier((source, same_one, same_two))

        def ff_blocks(w):
            return w.reshape(r, t, 2, 2, 2, h).transpose(2, 4, 0, 1, 3, 5).reshape(4, r, nb * h)

        pair = jnp.concatenate([ff_blocks(gate_weight), ff_blocks(up_weight)], axis=2)
        pair_mine = plane_swap(pair, member).reshape(4 * r, 2 * nb * h)
        pair_all = lax.all_gather(pair_mine, COLUMN)
        pair_full = pair_all.reshape(t, 2, 2, 2 * r, 2 * nb * h).transpose(0, 2, 1, 3, 4)
        pair_full = lax.optimization_barrier(pair_full.reshape(width, 2 * nb * h))
        down_full = lax.all_gather(down_weight, COLUMN, axis=0, tiled=True)
        dffn = jnp.concatenate(plane_gather(dffn_own))

        split = 4 * (3 * r + 16)
        head = conv_all[:, :split].reshape(t, 2, 2, 2, 3 * r + 16, share)
        in_full = head[:, :, :, :, : 3 * r].reshape(t, 2, 2, 2, 3, r, share)
        in_full = lax.optimization_barrier(
            in_full.transpose(0, 2, 1, 3, 5, 4, 6).reshape(width, 3 * share)
        )
        rest = head[:, :, :, :, 3 * r :].reshape(nb, 4, 16 * share)
        gains = rest[:, :, : 2 * r].reshape(t, 2, 2, 2, 2, r).transpose(4, 0, 2, 1, 3, 5)
        gains = gains.reshape(2, width).astype(F32)
        gains = lax.optimization_barrier(gains)
        gain_first, gain_second = gains[0], gains[1]
        kernel_vals = pick(rest.transpose(1, 0, 2), member)[:, 2 * r : 2 * r + taps * ch]
        kernel_vals = kernel_vals.reshape(nb, taps, ch).transpose(1, 0, 2).reshape(taps, share).astype(F32)
        out_full = conv_all[:, split:].reshape(nb, slabs, ch, LANES).transpose(0, 2, 1, 3)
        out_full, kernel_vals = lax.optimization_barrier((out_full.reshape(share, width), kernel_vals))

        scale_one = lax.rsqrt(jnp.mean(source * source, axis=1, keepdims=True) + EPS)
        normed_one = (source * scale_one * gain_first).astype(BF)
        projected = jnp.dot(normed_one, in_full, preferred_element_type=F32)
        projected = projected.reshape(4, slots, 3 * share)
        first = projected[:, :, :share]
        second = projected[:, :, share : 2 * share]
        stream = projected[:, :, 2 * share :]
        product = first * stream
        back_one = shifted(product, 1) * same_one
        back_two = shifted(product, 2) * same_two
        convolved = kernel_vals[0] * product + kernel_vals[1] * back_one + kernel_vals[2] * back_two
        mixer = (second * convolved).astype(BF).reshape(4 * slots, share)
        branch = jnp.dot(mixer, out_full, preferred_element_type=F32).reshape(4, slots, width)
        own = tokens.astype(F32)
        hidden = own + plane_sum(branch)

        scale_two = lax.rsqrt(jnp.mean(hidden * hidden, axis=1, keepdims=True) + EPS)
        normed_two_own = (hidden * scale_two * gain_second).astype(BF)
        normed_two = jnp.concatenate(plane_gather(normed_two_own))
        both = jnp.dot(normed_two, pair_full, preferred_element_type=F32)
        gate = both[:, : nb * h]
        upper = both[:, nb * h :]
        sigma = jax.nn.sigmoid(gate)
        swish = gate * sigma
        act = (swish * upper).astype(BF)
        dact = cols_by_cols(dffn, down_full)
        dgate = (dact * upper * sigma * (1.0 + gate * (1.0 - sigma))).astype(BF)
        dupper = (dact * swish).astype(BF)
        dboth = jnp.concatenate([dgate, dupper], axis=1)
        dnormed_two = plane_sum(cols_by_cols(dboth, pair_full).reshape(4, slots, width))
        down_grad = rows_by_rows(act, dffn).astype(BF)
        down_shard = lax.psum_scatter(down_grad, COLUMN, scatter_dimension=0, tiled=True).astype(F32)
        pair_grad = lax.optimization_barrier(rows_by_rows(normed_two, dboth).astype(BF))
        pair_grad = pair_grad.reshape(t, 2, 2, 2 * r, 2 * nb * h).transpose(0, 2, 1, 3, 4)
        pair_grad = lax.psum_scatter(pair_grad.reshape(nb, 4 * r, 2 * nb * h), COLUMN, scatter_dimension=0)
        ffn = plane_sum(jnp.dot(act, down_full, preferred_element_type=F32).reshape(4, slots, width))
        mixed = (live * (hidden + ffn)).astype(BF)
        hidden_part, gain_two_grad = norm_back(dnormed_two, hidden, scale_two, gain_second)
        dhidden = dout + hidden_part

        dbranch = jnp.concatenate(plane_gather(dhidden.astype(BF)))
        dmixer = cols_by_cols(dbranch, out_full).reshape(4, slots, share)
        dsecond = dmixer * convolved
        dconv = dmixer * second
        kernel_grad = jnp.stack(
            [
                jnp.sum(dconv * product, axis=(0, 1)),
                jnp.sum(dconv * back_one, axis=(0, 1)),
                jnp.sum(dconv * back_two, axis=(0, 1)),
            ]
        )
        dproduct = (
            kernel_vals[0] * dconv
            + kernel_vals[1] * lifted(dconv * same_one, 1)
            + kernel_vals[2] * lifted(dconv * same_two, 2)
        )
        dprojected = jnp.concatenate([dproduct * stream, dsecond, dproduct * first], axis=2)
        dprojected = dprojected.astype(BF).reshape(4 * slots, 3 * share)
        dnormed_part = cols_by_cols(dprojected, in_full)
        gain_one_grad = jnp.sum(dnormed_part * source * scale_one, axis=0)
        dnormed_one = plane_sum(dnormed_part.reshape(4, slots, width))
        own_scale = scale_one[:slots]
        weighted = dnormed_one * gain_first
        token_grad = (
            dhidden
            + own_scale * weighted
            - own * own_scale**3 * jnp.mean(weighted * own, axis=1, keepdims=True)
        )

        kernel_grad, gain_one_grad, gain_two_grad = lax.optimization_barrier(
            (kernel_grad, gain_one_grad, gain_two_grad)
        )
        in_grad = lax.optimization_barrier(rows_by_rows(normed_one, dprojected).astype(BF))
        in_grad = in_grad.reshape(t, 2, 2, 2, r, 3, share).transpose(0, 2, 1, 3, 5, 4, 6)
        in_grad = in_grad.reshape(nb, 4, 3 * r, share)
        gain_grads = jnp.stack([gain_one_grad, gain_two_grad]).astype(BF)
        gain_grads = gain_grads.reshape(2, t, 2, 2, 2, r).transpose(1, 3, 2, 4, 0, 5).reshape(nb, 4, 2 * r)
        gain_grads = jnp.pad(gain_grads, ((0, 0), (0, 0), (0, 16 * share - 2 * r)))
        in_grad = jnp.concatenate([in_grad, lax.optimization_barrier(gain_grads.reshape(nb, 4, 16, share))], axis=2)
        out_grad = lax.optimization_barrier(rows_by_rows(mixer, dbranch).astype(BF))
        out_grad = out_grad.reshape(nb, ch, slabs, LANES).transpose(0, 2, 1, 3).reshape(nb, slabs * ch, LANES)
        kernel_grad = kernel_grad.astype(BF).reshape(taps, nb, ch).transpose(1, 0, 2).reshape(nb, taps * ch)
        kernel_grad = jnp.pad(kernel_grad, ((0, 0), (0, 16 * share - taps * ch))).reshape(nb, 16, share)
        in_grad, out_grad, kernel_grad = lax.optimization_barrier(
            (in_grad.reshape(nb, split, share), out_grad, kernel_grad)
        )
        conv_grad = lax.optimization_barrier(jnp.concatenate([in_grad, out_grad, kernel_grad], axis=1))
        conv_grad = lax.psum_scatter(conv_grad, COLUMN, scatter_dimension=0)
        out_shard = conv_grad[split : split + slabs * ch].reshape(slabs, ch, LANES).transpose(1, 0, 2)
        out_shard = out_shard.reshape(ch, width).astype(F32)
        kernel_shard = conv_grad[split + slabs * ch :].reshape(-1)[: taps * ch].reshape(taps, ch).astype(F32)
        swapped = plane_swap(conv_grad[:split].reshape(4, 3 * r + 16, share), member)
        gain_shards = swapped[:, 3 * r :].reshape(4, 16 * share)[:, : 2 * r].astype(F32).sum(axis=0)
        in_shard = swapped[:, : 3 * r].reshape(2, 2, 3, r, t, 2, ch).transpose(3, 2, 4, 0, 5, 1, 6)
        in_shard = in_shard.reshape(r, 3 * width).astype(F32)
        pair_shard = plane_swap(pair_grad.reshape(4, r, 2 * nb * h), member)
        pair_shard = pair_shard.reshape(2, 2, r, 2, t, 2, h).transpose(3, 2, 4, 0, 5, 1, 6)
        pair_shard = pair_shard.reshape(2, r, 4 * nb * h).astype(F32)
        return (
            mixed,
            token_grad,
            gain_shards[:r],
            in_shard,
            kernel_shard,
            out_shard,
            gain_shards[r:],
            pair_shard[0],
            pair_shard[1],
            down_shard,
        )

    return local


def solution(mesh):
    t = mesh.shape["fsdp"] // 4
    grid = Mesh(mesh.devices.reshape(t, 2, 2, mesh.shape["rep"]), ("t", "b", "c", "y"))
    every = ("t", "b", "c", "y")
    in_specs = (
        P(every, None),
        P(every),
        P(every),
        P(every),
        P(every, None),
        P(None, every),
        P(every, None),
        P(every),
        P(every, None),
        P(every, None),
        P(every, None),
        P(every, None),
    )
    out_specs = (
        P(every, None),
        P(every, None),
        P(every),
        P(every, None),
        P(None, every),
        P(every, None),
        P(every),
        P(every, None),
        P(every, None),
        P(every, None),
    )
    return jax.shard_map(
        make_local(t), mesh=grid, in_specs=in_specs, out_specs=out_specs, check_vma=False
    )
```

```python
import jax
import jax.numpy as jnp
from jax import lax
from jax.sharding import Mesh, PartitionSpec as P

EPS = 1e-05
BF = jnp.bfloat16
F32 = jnp.float32

PLANE = ("b", "y")
COLUMN = ("t", "c")
LANES = 256


def rows_by_rows(left, right):
    return lax.dot_general(left, right, (((0,), (0,)), ((), ())), preferred_element_type=F32)


def cols_by_cols(left, right):
    return lax.dot_general(left, right, (((1,), (1,)), ((), ())), preferred_element_type=F32)


def to_peer(values, k):
    return lax.ppermute(values, PLANE, [(i, i ^ k) for i in range(4)])


def plane_gather(values):
    return [values] + [to_peer(values, k) for k in (1, 2, 3)]


def plane_sum(blocks):
    sent = [blocks[k].astype(BF) for k in (1, 2, 3)]
    total = blocks[0].astype(F32)
    for k in (1, 2, 3):
        total = total + to_peer(sent[k - 1], k).astype(F32)
    return total


def pick(blocks, i):
    return lax.dynamic_index_in_dim(blocks, i, 0, keepdims=False)


def plane_swap(blocks, member):
    got = [pick(blocks, member)] + [to_peer(pick(blocks, member ^ k), k) for k in (1, 2, 3)]
    got = jnp.stack(got)
    return jnp.stack([pick(got, member ^ j) for j in range(4)])


def after(values, other):
    one = other[(slice(0, 1),) * other.ndim].reshape(())
    return values + jnp.minimum(jnp.abs(one), 0).astype(values.dtype)


def norm_back(grad_norm, source, scale, gain):
    weighted = grad_norm * gain
    gain_grad = jnp.sum(grad_norm * source * scale, axis=0)
    source_grad = scale * weighted - source * scale**3 * jnp.mean(
        weighted * source, axis=1, keepdims=True
    )
    return (source_grad, gain_grad)


def shifted(values, steps):
    return jnp.pad(values, ((0, 0), (steps, 0), (0, 0)))[:, :-steps]


def lifted(values, steps):
    return jnp.pad(values, ((0, 0), (0, steps), (0, 0)))[:, steps:]


def make_local(t):
    nb = 2 * t

    def local(
        tokens,
        counts,
        segments,
        norm1_gain,
        in_weight,
        conv_kernel,
        out_weight,
        norm2_gain,
        gate_weight,
        up_weight,
        down_weight,
        cotangent,
    ):
        slots, width = tokens.shape
        r = in_weight.shape[0]
        ch = out_weight.shape[0]
        h = down_weight.shape[0]
        share = nb * ch
        taps = conv_kernel.shape[0]
        slabs = width // LANES
        member = 2 * lax.axis_index("b") + lax.axis_index("y")

        same_one = jnp.concatenate([jnp.zeros((1,), BF), (segments[1:] == segments[:-1]).astype(BF)])
        same_two = jnp.concatenate([jnp.zeros((2,), BF), (segments[2:] == segments[:-2]).astype(BF)])
        flags = jnp.concatenate([same_one, same_two])
        flags = jnp.pad(flags, (0, 16 * width - 2 * slots)).reshape(16, width)
        live = (jnp.arange(slots) < counts[0]).astype(F32)[:, None]
        dout = cotangent.astype(F32) * live
        dffn_own = dout.astype(BF)

        in_blocks = in_weight.reshape(r, 3, t, 2, 2, 2, ch).transpose(3, 5, 1, 0, 2, 4, 6)
        in_blocks = in_blocks.reshape(4, 3 * r, share)
        extra = jnp.concatenate([norm1_gain, norm2_gain, conv_kernel.reshape(-1)])
        extra = jnp.pad(extra, (0, 16 * share - extra.shape[0])).reshape(1, 16, share)
        conv_blocks = jnp.concatenate([in_blocks, jnp.broadcast_to(extra, (4, 16, share))], axis=1)
        conv_mine = plane_swap(conv_blocks, member)
        out_slabs = out_weight.reshape(ch, slabs, LANES).transpose(1, 0, 2).reshape(slabs * ch, LANES)
        conv_all = lax.all_gather(
            jnp.concatenate([conv_mine.reshape(4 * (3 * r + 16), share), out_slabs]), COLUMN
        )
        gathered = plane_gather(jnp.concatenate([tokens, flags]))
        source = jnp.stack([g[:slots] for g in gathered]).reshape(4 * slots, width).astype(F32)
        marks = jnp.stack([g[slots:].reshape(-1)[: 2 * slots] for g in gathered]).astype(F32)
        same_one = marks[:, :slots, None]
        same_two = marks[:, slots:, None]
        source, same_one, same_two = lax.optimization_barrier((source, same_one, same_two))

        def ff_blocks(w):
            return w.reshape(r, t, 2, 2, 2, h).transpose(2, 4, 0, 1, 3, 5).reshape(4, r, nb * h)

        pair = jnp.concatenate([ff_blocks(gate_weight), ff_blocks(up_weight)], axis=2)
        pair_mine = plane_swap(after(pair, gathered[3]), member).reshape(4 * r, 2 * nb * h)
        pair_all = lax.all_gather(pair_mine, COLUMN)
        pair_full = pair_all.reshape(t, 2, 2, 2 * r, 2 * nb * h).transpose(0, 2, 1, 3, 4)
        pair_full = lax.optimization_barrier(pair_full.reshape(width, 2 * nb * h))
        down_full = lax.all_gather(down_weight, COLUMN, axis=0, tiled=True)

        split = 4 * (3 * r + 16)
        head = conv_all[:, :split].reshape(t, 2, 2, 2, 3 * r + 16, share)
        in_full = head[:, :, :, :, : 3 * r].reshape(t, 2, 2, 2, 3, r, share)
        in_full = lax.optimization_barrier(
            in_full.transpose(0, 2, 1, 3, 5, 4, 6).reshape(width, 3 * share)
        )
        rest = head[:, :, :, :, 3 * r :].reshape(nb, 4, 16 * share)
        gains = rest[:, :, : 2 * r].reshape(t, 2, 2, 2, 2, r).transpose(4, 0, 2, 1, 3, 5)
        gains = gains.reshape(2, width).astype(F32)
        gains = lax.optimization_barrier(gains)
        gain_first, gain_second = gains[0], gains[1]
        kernel_vals = pick(rest.transpose(1, 0, 2), member)[:, 2 * r : 2 * r + taps * ch]
        kernel_vals = kernel_vals.reshape(nb, taps, ch).transpose(1, 0, 2).reshape(taps, share).astype(F32)
        out_full = conv_all[:, split:].reshape(nb, slabs, ch, LANES).transpose(0, 2, 1, 3)
        out_full, kernel_vals = lax.optimization_barrier((out_full.reshape(share, width), kernel_vals))

        scale_one = lax.rsqrt(jnp.mean(source * source, axis=1, keepdims=True) + EPS)
        normed_one = (source * scale_one * gain_first).astype(BF)
        projected = jnp.dot(normed_one, in_full, preferred_element_type=F32)
        projected = projected.reshape(4, slots, 3 * share)
        first = projected[:, :, :share]
        second = projected[:, :, share : 2 * share]
        stream = projected[:, :, 2 * share :]
        product = first * stream
        back_one = shifted(product, 1) * same_one
        back_two = shifted(product, 2) * same_two
        convolved = kernel_vals[0] * product + kernel_vals[1] * back_one + kernel_vals[2] * back_two
        mixer = (second * convolved).astype(BF).reshape(4 * slots, share)
        branch = jnp.dot(mixer, out_full, preferred_element_type=F32).reshape(4, slots, width)
        own = tokens.astype(F32)
        hidden = own + plane_sum(branch)

        scale_two = lax.rsqrt(jnp.mean(hidden * hidden, axis=1, keepdims=True) + EPS)
        normed_two_own = (hidden * scale_two * gain_second).astype(BF)
        normed_two = plane_gather(normed_two_own)
        dffn = jnp.concatenate(plane_gather(after(dffn_own, normed_two[3])))
        normed_two = jnp.concatenate(normed_two)
        both = jnp.dot(normed_two, pair_full, preferred_element_type=F32)
        gate = both[:, : nb * h]
        upper = both[:, nb * h :]
        sigma = jax.nn.sigmoid(gate)
        swish = gate * sigma
        act = (swish * upper).astype(BF)
        down_grad = rows_by_rows(act, dffn).astype(BF)
        down_sum = lax.psum_scatter(down_grad, COLUMN, scatter_dimension=0, tiled=True)
        down_shard = down_sum.astype(F32)
        dact = after(cols_by_cols(dffn, down_full), down_grad)
        dgate = (dact * upper * sigma * (1.0 + gate * (1.0 - sigma))).astype(BF)
        dupper = (dact * swish).astype(BF)
        dboth = jnp.concatenate([dgate, dupper], axis=1)
        dnormed_part = cols_by_cols(dboth, pair_full).reshape(4, slots, width)
        pair_grad = after(rows_by_rows(normed_two, dboth), dnormed_part)
        pair_grad = lax.optimization_barrier(pair_grad.astype(BF))
        pair_grad = pair_grad.reshape(t, 2, 2, 2 * r, 2 * nb * h).transpose(0, 2, 1, 3, 4)
        pair_grad = after(pair_grad.reshape(nb, 4 * r, 2 * nb * h), down_sum)
        pair_sum = lax.psum_scatter(pair_grad, COLUMN, scatter_dimension=0)
        dnormed_two = after(plane_sum(dnormed_part), pair_grad)
        hidden_part, gain_two_grad = norm_back(dnormed_two, hidden, scale_two, gain_second)
        dhidden = dout + hidden_part

        dbranch = plane_gather(dhidden.astype(BF))
        dbranch_last = dbranch[3]
        dbranch = jnp.concatenate(dbranch)
        ffn = after(jnp.dot(act, down_full, preferred_element_type=F32), dbranch_last)
        ffn = plane_sum(ffn.reshape(4, slots, width))
        mixed = (live * (hidden + ffn)).astype(BF)
        dmixer = cols_by_cols(dbranch, out_full).reshape(4, slots, share)
        dsecond = dmixer * convolved
        dconv = dmixer * second
        kernel_grad = jnp.stack(
            [
                jnp.sum(dconv * product, axis=(0, 1)),
                jnp.sum(dconv * back_one, axis=(0, 1)),
                jnp.sum(dconv * back_two, axis=(0, 1)),
            ]
        )
        dproduct = (
            kernel_vals[0] * dconv
            + kernel_vals[1] * lifted(dconv * same_one, 1)
            + kernel_vals[2] * lifted(dconv * same_two, 2)
        )
        dprojected = jnp.concatenate([dproduct * stream, dsecond, dproduct * first], axis=2)
        dprojected = dprojected.astype(BF).reshape(4 * slots, 3 * share)
        dnormed_part = cols_by_cols(dprojected, in_full)
        gain_one_grad = jnp.sum(dnormed_part * source * scale_one, axis=0)
        dnormed_one = plane_sum(dnormed_part.reshape(4, slots, width))
        own_scale = scale_one[:slots]
        weighted = dnormed_one * gain_first
        token_grad = (
            dhidden
            + own_scale * weighted
            - own * own_scale**3 * jnp.mean(weighted * own, axis=1, keepdims=True)
        )

        kernel_grad, gain_one_grad, gain_two_grad = lax.optimization_barrier(
            (kernel_grad, gain_one_grad, gain_two_grad)
        )
        in_grad = lax.optimization_barrier(rows_by_rows(normed_one, dprojected).astype(BF))
        in_grad = jnp.stack(
            [
                in_grad[:, i * share : (i + 1) * share].reshape(t, 2, 2, 2, r, share).transpose(0, 2, 1, 3, 4, 5)
                for i in range(3)
            ],
            axis=4,
        )
        in_grad = in_grad.reshape(nb, 4, 3 * r, share)
        gain_grads = jnp.stack([gain_one_grad, gain_two_grad]).astype(BF)
        gain_grads = gain_grads.reshape(2, t, 2, 2, 2, r).transpose(1, 3, 2, 4, 0, 5).reshape(nb, 4, 2 * r)
        gain_grads = jnp.pad(gain_grads, ((0, 0), (0, 0), (0, 16 * share - 2 * r)))
        in_grad = jnp.concatenate([in_grad, lax.optimization_barrier(gain_grads.reshape(nb, 4, 16, share))], axis=2)
        out_grad = lax.optimization_barrier(rows_by_rows(mixer, dbranch).astype(BF))
        out_grad = jnp.concatenate(
            [out_grad[:, i * LANES : (i + 1) * LANES].reshape(nb, ch, LANES) for i in range(slabs)], axis=1
        )
        kernel_grad = kernel_grad.astype(BF).reshape(taps, nb, ch).transpose(1, 0, 2).reshape(nb, taps * ch)
        kernel_grad = jnp.pad(kernel_grad, ((0, 0), (0, 16 * share - taps * ch))).reshape(nb, 16, share)
        in_grad, out_grad, kernel_grad = lax.optimization_barrier(
            (in_grad.reshape(nb, split, share), out_grad, kernel_grad)
        )
        conv_grad = after(jnp.concatenate([in_grad, out_grad, kernel_grad], axis=1), pair_sum)
        conv_grad = lax.psum_scatter(conv_grad, COLUMN, scatter_dimension=0)
        out_shard = conv_grad[split : split + slabs * ch].reshape(slabs, ch, LANES).transpose(1, 0, 2)
        out_shard = out_shard.reshape(ch, width).astype(F32)
        kernel_shard = conv_grad[split + slabs * ch :].reshape(-1)[: taps * ch].reshape(taps, ch).astype(F32)
        swapped = plane_swap(conv_grad[:split].reshape(4, 3 * r + 16, share), member)
        gain_shards = swapped[:, 3 * r :].reshape(4, 16 * share)[:, : 2 * r].astype(F32).sum(axis=0)
        in_shard = swapped[:, : 3 * r].reshape(2, 2, 3, r, t, 2, ch).transpose(3, 2, 4, 0, 5, 1, 6)
        in_shard = in_shard.reshape(r, 3 * width).astype(F32)
        pair_shard = plane_swap(pair_sum.reshape(4, r, 2 * nb * h), member)
        pair_shard = pair_shard.reshape(2, 2, r, 2, t, 2, h).transpose(3, 2, 4, 0, 5, 1, 6)
        pair_shard = pair_shard.reshape(2, r, 4 * nb * h).astype(F32)
        return (
            mixed,
            token_grad,
            gain_shards[:r],
            in_shard,
            kernel_shard,
            out_shard,
            gain_shards[r:],
            pair_shard[0],
            pair_shard[1],
            down_shard,
        )

    return local


def solution(mesh):
    t = mesh.shape["fsdp"] // 4
    grid = Mesh(mesh.devices.reshape(t, 2, 2, mesh.shape["rep"]), ("t", "b", "c", "y"))
    every = ("t", "b", "c", "y")
    in_specs = (
        P(every, None),
        P(every),
        P(every),
        P(every),
        P(every, None),
        P(None, every),
        P(every, None),
        P(every),
        P(every, None),
        P(every, None),
        P(every, None),
        P(every, None),
    )
    out_specs = (
        P(every, None),
        P(every, None),
        P(every),
        P(every, None),
        P(None, every),
        P(every, None),
        P(every),
        P(every, None),
        P(every, None),
        P(every, None),
    )
    return jax.shard_map(
        make_local(t), mesh=grid, in_specs=in_specs, out_specs=out_specs, check_vma=False
    )
```

```python
import jax
import jax.numpy as jnp
from jax import lax
from jax.sharding import Mesh, PartitionSpec as P

EPS = 1e-05
BF = jnp.bfloat16
F32 = jnp.float32

PLANE = ("b", "y")
COLUMN = ("t", "c")
LANES = 256


def rows_by_rows(left, right):
    return lax.dot_general(left, right, (((0,), (0,)), ((), ())), preferred_element_type=F32)


def cols_by_cols(left, right):
    return lax.dot_general(left, right, (((1,), (1,)), ((), ())), preferred_element_type=F32)


def to_peer(values, k):
    return lax.ppermute(values, PLANE, [(i, i ^ k) for i in range(4)])


def plane_gather(values):
    return [values] + [to_peer(values, k) for k in (1, 2, 3)]


def plane_sum(blocks, *others):
    sent = [after(blocks[k].astype(BF), *others) for k in (1, 2, 3)]
    total = blocks[0].astype(F32)
    for k in (1, 2, 3):
        total = total + to_peer(sent[k - 1], k).astype(F32)
    return total


def pick(blocks, i):
    return lax.dynamic_index_in_dim(blocks, i, 0, keepdims=False)


def plane_swap(blocks, member):
    got = [pick(blocks, member)] + [to_peer(pick(blocks, member ^ k), k) for k in (1, 2, 3)]
    got = jnp.stack(got)
    return jnp.stack([pick(got, member ^ j) for j in range(4)])


def after(values, *others):
    for other in others:
        one = other[(slice(0, 1),) * other.ndim].reshape(())
        values = values + jnp.minimum(jnp.abs(one), 0).astype(values.dtype)
    return values


def norm_back(grad_norm, source, scale, gain):
    weighted = grad_norm * gain
    gain_grad = jnp.sum(grad_norm * source * scale, axis=0)
    source_grad = scale * weighted - source * scale**3 * jnp.mean(
        weighted * source, axis=1, keepdims=True
    )
    return (source_grad, gain_grad)


def shifted(values, steps):
    return jnp.pad(values, ((0, 0), (steps, 0), (0, 0)))[:, :-steps]


def lifted(values, steps):
    return jnp.pad(values, ((0, 0), (0, steps), (0, 0)))[:, steps:]


def make_local(t):
    nb = 2 * t

    def local(
        tokens,
        counts,
        segments,
        norm1_gain,
        in_weight,
        conv_kernel,
        out_weight,
        norm2_gain,
        gate_weight,
        up_weight,
        down_weight,
        cotangent,
    ):
        slots, width = tokens.shape
        r = in_weight.shape[0]
        ch = out_weight.shape[0]
        h = down_weight.shape[0]
        share = nb * ch
        taps = conv_kernel.shape[0]
        slabs = width // LANES
        member = 2 * lax.axis_index("b") + lax.axis_index("y")

        same_one = jnp.concatenate([jnp.zeros((1,), BF), (segments[1:] == segments[:-1]).astype(BF)])
        same_two = jnp.concatenate([jnp.zeros((2,), BF), (segments[2:] == segments[:-2]).astype(BF)])
        flags = jnp.concatenate([same_one, same_two])
        flags = jnp.pad(flags, (0, 16 * width - 2 * slots)).reshape(16, width)
        live = (jnp.arange(slots) < counts[0]).astype(F32)[:, None]
        dout = cotangent.astype(F32) * live
        dffn_own = dout.astype(BF)

        in_blocks = in_weight.reshape(r, 3, t, 2, 2, 2, ch).transpose(3, 5, 1, 0, 2, 4, 6)
        in_blocks = in_blocks.reshape(4, 3 * r, share)
        extra = jnp.concatenate([norm1_gain, norm2_gain, conv_kernel.reshape(-1)])
        extra = jnp.pad(extra, (0, 16 * share - extra.shape[0])).reshape(1, 16, share)
        conv_blocks = jnp.concatenate([in_blocks, jnp.broadcast_to(extra, (4, 16, share))], axis=1)
        conv_mine = plane_swap(conv_blocks, member)
        out_slabs = out_weight.reshape(ch, slabs, LANES).transpose(1, 0, 2).reshape(slabs * ch, LANES)
        conv_all = lax.all_gather(
            jnp.concatenate([conv_mine.reshape(4 * (3 * r + 16), share), out_slabs]), COLUMN
        )
        gathered = plane_gather(jnp.concatenate([tokens, flags]))
        source = jnp.stack([g[:slots] for g in gathered]).reshape(4 * slots, width).astype(F32)
        marks = jnp.stack([g[slots:].reshape(-1)[: 2 * slots] for g in gathered]).astype(F32)
        same_one = marks[:, :slots, None]
        same_two = marks[:, slots:, None]
        source, same_one, same_two = lax.optimization_barrier((source, same_one, same_two))

        def ff_blocks(w):
            return w.reshape(r, t, 2, 2, 2, h).transpose(2, 4, 0, 1, 3, 5).reshape(4, r, nb * h)

        pair = jnp.concatenate([ff_blocks(gate_weight), ff_blocks(up_weight)], axis=2)
        pair_mine = plane_swap(after(pair, *gathered[1:]), member).reshape(4 * r, 2 * nb * h)
        pair_all = lax.all_gather(pair_mine, COLUMN)
        pair_full = pair_all.reshape(t, 2, 2, 2 * r, 2 * nb * h).transpose(0, 2, 1, 3, 4)
        pair_full = lax.optimization_barrier(pair_full.reshape(width, 2 * nb * h))
        down_full = lax.all_gather(down_weight, COLUMN, axis=0, tiled=True)

        split = 4 * (3 * r + 16)
        head = conv_all[:, :split].reshape(t, 2, 2, 2, 3 * r + 16, share)
        in_full = head[:, :, :, :, : 3 * r].reshape(t, 2, 2, 2, 3, r, share)
        in_full = lax.optimization_barrier(
            in_full.transpose(0, 2, 1, 3, 5, 4, 6).reshape(width, 3 * share)
        )
        rest = head[:, :, :, :, 3 * r :].reshape(nb, 4, 16 * share)
        gains = rest[:, :, : 2 * r].reshape(t, 2, 2, 2, 2, r).transpose(4, 0, 2, 1, 3, 5)
        gains = gains.reshape(2, width).astype(F32)
        gains = lax.optimization_barrier(gains)
        gain_first, gain_second = gains[0], gains[1]
        kernel_vals = pick(rest.transpose(1, 0, 2), member)[:, 2 * r : 2 * r + taps * ch]
        kernel_vals = kernel_vals.reshape(nb, taps, ch).transpose(1, 0, 2).reshape(taps, share).astype(F32)
        out_full = conv_all[:, split:].reshape(nb, slabs, ch, LANES).transpose(0, 2, 1, 3)
        out_full, kernel_vals = lax.optimization_barrier((out_full.reshape(share, width), kernel_vals))

        scale_one = lax.rsqrt(jnp.mean(source * source, axis=1, keepdims=True) + EPS)
        normed_one = (source * scale_one * gain_first).astype(BF)
        projected = jnp.dot(normed_one, in_full, preferred_element_type=F32)
        projected = projected.reshape(4, slots, 3 * share)
        first = projected[:, :, :share]
        second = projected[:, :, share : 2 * share]
        stream = projected[:, :, 2 * share :]
        product = first * stream
        back_one = shifted(product, 1) * same_one
        back_two = shifted(product, 2) * same_two
        convolved = kernel_vals[0] * product + kernel_vals[1] * back_one + kernel_vals[2] * back_two
        mixer = (second * convolved).astype(BF).reshape(4 * slots, share)
        branch = jnp.dot(mixer, out_full, preferred_element_type=F32).reshape(4, slots, width)
        dffn = plane_gather(after(dffn_own, conv_all))
        own = tokens.astype(F32)
        hidden = own + plane_sum(branch, *dffn[1:])
        dffn = jnp.concatenate(dffn)

        scale_two = lax.rsqrt(jnp.mean(hidden * hidden, axis=1, keepdims=True) + EPS)
        normed_two_own = (hidden * scale_two * gain_second).astype(BF)
        normed_two = plane_gather(normed_two_own)
        normed_two = jnp.concatenate(normed_two)
        both = jnp.dot(normed_two, pair_full, preferred_element_type=F32)
        gate = both[:, : nb * h]
        upper = both[:, nb * h :]
        sigma = jax.nn.sigmoid(gate)
        swish = gate * sigma
        act = (swish * upper).astype(BF)
        down_grad = rows_by_rows(act, dffn).astype(BF)
        down_sum = lax.psum_scatter(down_grad, COLUMN, scatter_dimension=0, tiled=True)
        down_shard = down_sum.astype(F32)
        dact = after(cols_by_cols(dffn, down_full), down_grad)
        dgate = (dact * upper * sigma * (1.0 + gate * (1.0 - sigma))).astype(BF)
        dupper = (dact * swish).astype(BF)
        dboth = jnp.concatenate([dgate, dupper], axis=1)
        dnormed_part = cols_by_cols(dboth, pair_full).reshape(4, slots, width)
        pair_grad = after(rows_by_rows(normed_two, dboth), dnormed_part)
        pair_grad = lax.optimization_barrier(pair_grad.astype(BF))
        pair_grad = pair_grad.reshape(t, 2, 2, 2 * r, 2 * nb * h).transpose(0, 2, 1, 3, 4)
        pair_grad = after(pair_grad.reshape(nb, 4 * r, 2 * nb * h), down_sum)
        pair_sum = lax.psum_scatter(pair_grad, COLUMN, scatter_dimension=0)
        dnormed_two = plane_sum(dnormed_part)
        hidden_part, gain_two_grad = norm_back(dnormed_two, hidden, scale_two, gain_second)
        dhidden = dout + hidden_part

        dbranch = plane_gather(after(dhidden.astype(BF), pair_grad))
        dbranch_parts = dbranch[1:]
        dbranch = jnp.concatenate(dbranch)
        ffn = jnp.dot(act, down_full, preferred_element_type=F32).reshape(4, slots, width)
        ffn = plane_sum(lax.optimization_barrier(ffn), *dbranch_parts)
        mixed = (live * (hidden + ffn)).astype(BF)
        dmixer = cols_by_cols(dbranch, out_full).reshape(4, slots, share)
        dsecond = dmixer * convolved
        dconv = dmixer * second
        kernel_grad = jnp.stack(
            [
                jnp.sum(dconv * product, axis=(0, 1)),
                jnp.sum(dconv * back_one, axis=(0, 1)),
                jnp.sum(dconv * back_two, axis=(0, 1)),
            ]
        )
        dproduct = (
            kernel_vals[0] * dconv
            + kernel_vals[1] * lifted(dconv * same_one, 1)
            + kernel_vals[2] * lifted(dconv * same_two, 2)
        )
        dprojected = jnp.concatenate([dproduct * stream, dsecond, dproduct * first], axis=2)
        dprojected = dprojected.astype(BF).reshape(4 * slots, 3 * share)
        dnormed_part = cols_by_cols(dprojected, in_full)
        gain_one_grad = jnp.sum(dnormed_part * source * scale_one, axis=0)
        dnormed_one = plane_sum(dnormed_part.reshape(4, slots, width))
        own_scale = scale_one[:slots]
        weighted = dnormed_one * gain_first
        token_grad = (
            dhidden
            + own_scale * weighted
            - own * own_scale**3 * jnp.mean(weighted * own, axis=1, keepdims=True)
        )

        kernel_grad, gain_one_grad, gain_two_grad = lax.optimization_barrier(
            (kernel_grad, gain_one_grad, gain_two_grad)
        )
        in_grad = lax.optimization_barrier(rows_by_rows(normed_one, dprojected).astype(BF))
        in_grad = jnp.stack(
            [
                in_grad[:, i * share : (i + 1) * share].reshape(t, 2, 2, 2, r, share).transpose(0, 2, 1, 3, 4, 5)
                for i in range(3)
            ],
            axis=4,
        )
        in_grad = in_grad.reshape(nb, 4, 3 * r, share)
        gain_grads = jnp.stack([gain_one_grad, gain_two_grad]).astype(BF)
        gain_grads = gain_grads.reshape(2, t, 2, 2, 2, r).transpose(1, 3, 2, 4, 0, 5).reshape(nb, 4, 2 * r)
        gain_grads = jnp.pad(gain_grads, ((0, 0), (0, 0), (0, 16 * share - 2 * r)))
        in_grad = jnp.concatenate([in_grad, lax.optimization_barrier(gain_grads.reshape(nb, 4, 16, share))], axis=2)
        out_grad = lax.optimization_barrier(rows_by_rows(mixer, dbranch).astype(BF))
        out_grad = jnp.concatenate(
            [out_grad[:, i * LANES : (i + 1) * LANES].reshape(nb, ch, LANES) for i in range(slabs)], axis=1
        )
        kernel_grad = kernel_grad.astype(BF).reshape(taps, nb, ch).transpose(1, 0, 2).reshape(nb, taps * ch)
        kernel_grad = jnp.pad(kernel_grad, ((0, 0), (0, 16 * share - taps * ch))).reshape(nb, 16, share)
        in_grad, out_grad, kernel_grad = lax.optimization_barrier(
            (in_grad.reshape(nb, split, share), out_grad, kernel_grad)
        )
        conv_grad = after(jnp.concatenate([in_grad, out_grad, kernel_grad], axis=1), pair_sum)
        conv_grad = lax.psum_scatter(conv_grad, COLUMN, scatter_dimension=0)
        out_shard = conv_grad[split : split + slabs * ch].reshape(slabs, ch, LANES).transpose(1, 0, 2)
        out_shard = out_shard.reshape(ch, width).astype(F32)
        kernel_shard = conv_grad[split + slabs * ch :].reshape(-1)[: taps * ch].reshape(taps, ch).astype(F32)
        swapped = plane_swap(conv_grad[:split].reshape(4, 3 * r + 16, share), member)
        gain_shards = swapped[:, 3 * r :].reshape(4, 16 * share)[:, : 2 * r].astype(F32).sum(axis=0)
        in_shard = swapped[:, : 3 * r].reshape(2, 2, 3, r, t, 2, ch).transpose(3, 2, 4, 0, 5, 1, 6)
        in_shard = in_shard.reshape(r, 3 * width).astype(F32)
        pair_shard = plane_swap(pair_sum.reshape(4, r, 2 * nb * h), member)
        pair_shard = pair_shard.reshape(2, 2, r, 2, t, 2, h).transpose(3, 2, 4, 0, 5, 1, 6)
        pair_shard = pair_shard.reshape(2, r, 4 * nb * h).astype(F32)
        return (
            mixed,
            token_grad,
            gain_shards[:r],
            in_shard,
            kernel_shard,
            out_shard,
            gain_shards[r:],
            pair_shard[0],
            pair_shard[1],
            down_shard,
        )

    return local


def solution(mesh):
    t = mesh.shape["fsdp"] // 4
    grid = Mesh(mesh.devices.reshape(t, 2, 2, mesh.shape["rep"]), ("t", "b", "c", "y"))
    every = ("t", "b", "c", "y")
    in_specs = (
        P(every, None),
        P(every),
        P(every),
        P(every),
        P(every, None),
        P(None, every),
        P(every, None),
        P(every),
        P(every, None),
        P(every, None),
        P(every, None),
        P(every, None),
    )
    out_specs = (
        P(every, None),
        P(every, None),
        P(every),
        P(every, None),
        P(None, every),
        P(every, None),
        P(every),
        P(every, None),
        P(every, None),
        P(every, None),
    )
    return jax.shard_map(
        make_local(t), mesh=grid, in_specs=in_specs, out_specs=out_specs, check_vma=False
    )
```

```python
import jax
import jax.numpy as jnp
from jax import lax
from jax.sharding import Mesh, PartitionSpec as P

EPS = 1e-05
BF = jnp.bfloat16
F32 = jnp.float32

PLANE = ("b", "y")
COLUMN = ("t", "c")
LANES = 256


def rows_by_rows(left, right):
    return lax.dot_general(left, right, (((0,), (0,)), ((), ())), preferred_element_type=F32)


def cols_by_cols(left, right):
    return lax.dot_general(left, right, (((1,), (1,)), ((), ())), preferred_element_type=F32)


def to_peer(values, k):
    return lax.ppermute(values, PLANE, [(i, i ^ k) for i in range(4)])


def plane_gather(values):
    return [values] + [to_peer(values, k) for k in (1, 2, 3)]


def plane_sum(blocks, *others):
    sent = [after(blocks[k].astype(BF), *others) for k in (1, 2, 3)]
    total = blocks[0].astype(F32)
    for k in (1, 2, 3):
        total = total + to_peer(sent[k - 1], k).astype(F32)
    return total


def pick(blocks, i):
    return lax.dynamic_index_in_dim(blocks, i, 0, keepdims=False)


def plane_swap(blocks, member):
    got = [pick(blocks, member)] + [to_peer(pick(blocks, member ^ k), k) for k in (1, 2, 3)]
    got = jnp.stack(got)
    return jnp.stack([pick(got, member ^ j) for j in range(4)])


def after(values, *others):
    for other in others:
        if other.shape != values.shape:
            other = other[(slice(0, 1),) * other.ndim].reshape(())
        values = values + jnp.minimum(jnp.abs(other), 0).astype(values.dtype)
    return values


def norm_back(grad_norm, source, scale, gain):
    weighted = grad_norm * gain
    gain_grad = jnp.sum(grad_norm * source * scale, axis=0)
    row_mean = jnp.mean(weighted * source, axis=1, keepdims=True)
    source_grad = scale * weighted - source * scale**3 * row_mean
    return (source_grad, gain_grad, row_mean)


def shifted(values, steps):
    return jnp.pad(values, ((0, 0), (steps, 0), (0, 0)))[:, :-steps]


def lifted(values, steps):
    return jnp.pad(values, ((0, 0), (0, steps), (0, 0)))[:, steps:]


def make_local(t):
    nb = 2 * t

    def local(
        tokens,
        counts,
        segments,
        norm1_gain,
        in_weight,
        conv_kernel,
        out_weight,
        norm2_gain,
        gate_weight,
        up_weight,
        down_weight,
        cotangent,
    ):
        slots, width = tokens.shape
        r = in_weight.shape[0]
        ch = out_weight.shape[0]
        h = down_weight.shape[0]
        share = nb * ch
        taps = conv_kernel.shape[0]
        slabs = width // LANES
        member = 2 * lax.axis_index("b") + lax.axis_index("y")

        same_one = jnp.concatenate([jnp.zeros((1,), BF), (segments[1:] == segments[:-1]).astype(BF)])
        same_two = jnp.concatenate([jnp.zeros((2,), BF), (segments[2:] == segments[:-2]).astype(BF)])
        flags = jnp.concatenate([same_one, same_two])
        flags = jnp.pad(flags, (0, 16 * width - 2 * slots)).reshape(16, width)
        live = (jnp.arange(slots) < counts[0]).astype(F32)[:, None]
        dout = cotangent.astype(F32) * live
        dffn_own = dout.astype(BF)

        in_blocks = in_weight.reshape(r, 3, t, 2, 2, 2, ch).transpose(3, 5, 1, 0, 2, 4, 6)
        in_blocks = in_blocks.reshape(4, 3 * r, share)
        extra = jnp.concatenate([norm1_gain, norm2_gain, conv_kernel.reshape(-1)])
        extra = jnp.pad(extra, (0, 16 * share - extra.shape[0])).reshape(1, 16, share)
        conv_blocks = jnp.concatenate([in_blocks, jnp.broadcast_to(extra, (4, 16, share))], axis=1)
        conv_mine = plane_swap(conv_blocks, member)
        out_slabs = out_weight.reshape(ch, slabs, LANES).transpose(1, 0, 2).reshape(slabs * ch, LANES)
        conv_all = lax.all_gather(
            jnp.concatenate([conv_mine.reshape(4 * (3 * r + 16), share), out_slabs]), COLUMN
        )
        gathered = plane_gather(jnp.concatenate([tokens, flags]))
        source = jnp.stack([g[:slots] for g in gathered]).reshape(4 * slots, width).astype(F32)
        marks = jnp.stack([g[slots:].reshape(-1)[: 2 * slots] for g in gathered]).astype(F32)
        same_one = marks[:, :slots, None]
        same_two = marks[:, slots:, None]
        source, same_one, same_two = lax.optimization_barrier((source, same_one, same_two))

        def ff_blocks(w):
            return w.reshape(r, t, 2, 2, 2, h).transpose(2, 4, 0, 1, 3, 5).reshape(4, r, nb * h)

        tile = sum(g[:16, :128] for g in gathered[1:])
        pair = after(jnp.concatenate([ff_blocks(gate_weight), ff_blocks(up_weight)], axis=2), tile)
        pair_mine = plane_swap(pair, member).reshape(4 * r, 2 * nb * h)
        dffn = plane_gather(after(dffn_own, *[g[:slots] for g in gathered[1:]]))
        pair_all = lax.all_gather(pair_mine, COLUMN)
        pair_full = pair_all.reshape(t, 2, 2, 2 * r, 2 * nb * h).transpose(0, 2, 1, 3, 4)
        pair_full = lax.optimization_barrier(pair_full.reshape(width, 2 * nb * h))
        down_full = lax.all_gather(down_weight, COLUMN, axis=0, tiled=True)

        split = 4 * (3 * r + 16)
        head = conv_all[:, :split].reshape(t, 2, 2, 2, 3 * r + 16, share)
        in_full = head[:, :, :, :, : 3 * r].reshape(t, 2, 2, 2, 3, r, share)
        in_full = lax.optimization_barrier(
            in_full.transpose(0, 2, 1, 3, 5, 4, 6).reshape(width, 3 * share)
        )
        rest = head[:, :, :, :, 3 * r :].reshape(nb, 4, 16 * share)
        gains = rest[:, :, : 2 * r].reshape(t, 2, 2, 2, 2, r).transpose(4, 0, 2, 1, 3, 5)
        gains = gains.reshape(2, width).astype(F32)
        gains = lax.optimization_barrier(gains)
        gain_first, gain_second = gains[0], gains[1]
        kernel_vals = pick(rest.transpose(1, 0, 2), member)[:, 2 * r : 2 * r + taps * ch]
        kernel_vals = kernel_vals.reshape(nb, taps, ch).transpose(1, 0, 2).reshape(taps, share).astype(F32)
        out_full = conv_all[:, split:].reshape(nb, slabs, ch, LANES).transpose(0, 2, 1, 3)
        out_full, kernel_vals = lax.optimization_barrier((out_full.reshape(share, width), kernel_vals))

        scale_one = lax.rsqrt(jnp.mean(source * source, axis=1, keepdims=True) + EPS)
        normed_one = (source * scale_one * gain_first).astype(BF)
        projected = jnp.dot(normed_one, in_full, preferred_element_type=F32)
        projected = projected.reshape(4, slots, 3 * share)
        first = projected[:, :, :share]
        second = projected[:, :, share : 2 * share]
        stream = projected[:, :, 2 * share :]
        product = first * stream
        back_one = shifted(product, 1) * same_one
        back_two = shifted(product, 2) * same_two
        convolved = kernel_vals[0] * product + kernel_vals[1] * back_one + kernel_vals[2] * back_two
        mixer = (second * convolved).astype(BF).reshape(4 * slots, share)
        branch = jnp.dot(mixer, out_full, preferred_element_type=F32).reshape(4, slots, width)
        own = tokens.astype(F32)
        hidden = own + plane_sum(branch, *dffn[1:])
        dffn = jnp.concatenate(dffn)

        scale_two = lax.rsqrt(jnp.mean(hidden * hidden, axis=1, keepdims=True) + EPS)
        normed_two_own = (hidden * scale_two * gain_second).astype(BF)
        normed_two = plane_gather(normed_two_own)
        normed_two = jnp.concatenate(normed_two)
        both = jnp.dot(normed_two, pair_full, preferred_element_type=F32)
        gate = both[:, : nb * h]
        upper = both[:, nb * h :]
        sigma = jax.nn.sigmoid(gate)
        swish = gate * sigma
        act = (swish * upper).astype(BF)
        down_grad = rows_by_rows(act, dffn).astype(BF)
        down_sum = lax.psum_scatter(down_grad, COLUMN, scatter_dimension=0, tiled=True)
        down_shard = down_sum.astype(F32)
        dact = after(cols_by_cols(dffn, down_full), down_grad)
        dgate = (dact * upper * sigma * (1.0 + gate * (1.0 - sigma))).astype(BF)
        dupper = (dact * swish).astype(BF)
        dboth = jnp.concatenate([dgate, dupper], axis=1)
        dnormed_part = cols_by_cols(dboth, pair_full).reshape(4, slots, width)
        pair_grad = lax.optimization_barrier(rows_by_rows(normed_two, dboth).astype(BF))
        dnormed_two = plane_sum(dnormed_part)
        hidden_part, gain_two_grad, row_mean = norm_back(dnormed_two, hidden, scale_two, gain_second)
        pair_grad = pair_grad.reshape(t, 2, 2, 2 * r, 2 * nb * h).transpose(0, 2, 1, 3, 4)
        pair_grad = after(pair_grad.reshape(nb, 4 * r, 2 * nb * h), down_sum, row_mean)
        pair_sum = lax.psum_scatter(pair_grad, COLUMN, scatter_dimension=0)
        dhidden = dout + hidden_part

        dbranch = plane_gather(dhidden.astype(BF))
        dbranch_parts = dbranch[1:]
        dbranch = jnp.concatenate(dbranch)
        ffn = jnp.dot(act, down_full, preferred_element_type=F32).reshape(4, slots, width)
        ffn = plane_sum(lax.optimization_barrier(ffn), *dbranch_parts)
        mixed = (live * (hidden + ffn)).astype(BF)
        dmixer = cols_by_cols(dbranch, out_full).reshape(4, slots, share)
        dsecond = dmixer * convolved
        dconv = dmixer * second
        kernel_grad = jnp.stack(
            [
                jnp.sum(dconv * product, axis=(0, 1)),
                jnp.sum(dconv * back_one, axis=(0, 1)),
                jnp.sum(dconv * back_two, axis=(0, 1)),
            ]
        )
        dproduct = (
            kernel_vals[0] * dconv
            + kernel_vals[1] * lifted(dconv * same_one, 1)
            + kernel_vals[2] * lifted(dconv * same_two, 2)
        )
        dprojected = jnp.concatenate([dproduct * stream, dsecond, dproduct * first], axis=2)
        dprojected = dprojected.astype(BF).reshape(4 * slots, 3 * share)
        dnormed_part = after(cols_by_cols(dprojected, in_full), mixed[:16, :128])
        gain_one_grad = jnp.sum(dnormed_part * source * scale_one, axis=0)
        pair_shard = plane_swap(pair_sum.reshape(4, r, 2 * nb * h), member)
        dnormed_one = plane_sum(dnormed_part.reshape(4, slots, width), pair_shard[3])
        own_scale = scale_one[:slots]
        weighted = dnormed_one * gain_first
        token_grad = (
            dhidden
            + own_scale * weighted
            - own * own_scale**3 * jnp.mean(weighted * own, axis=1, keepdims=True)
        )

        kernel_grad, gain_one_grad, gain_two_grad = lax.optimization_barrier(
            (kernel_grad, gain_one_grad, gain_two_grad)
        )
        in_grad = lax.optimization_barrier(rows_by_rows(normed_one, dprojected).astype(BF))
        in_grad = jnp.stack(
            [
                in_grad[:, i * share : (i + 1) * share].reshape(t, 2, 2, 2, r, share).transpose(0, 2, 1, 3, 4, 5)
                for i in range(3)
            ],
            axis=4,
        )
        in_grad = in_grad.reshape(nb, 4, 3 * r, share)
        gain_grads = jnp.stack([gain_one_grad, gain_two_grad]).astype(BF)
        gain_grads = gain_grads.reshape(2, t, 2, 2, 2, r).transpose(1, 3, 2, 4, 0, 5).reshape(nb, 4, 2 * r)
        gain_grads = jnp.pad(gain_grads, ((0, 0), (0, 0), (0, 16 * share - 2 * r)))
        in_grad = jnp.concatenate([in_grad, lax.optimization_barrier(gain_grads.reshape(nb, 4, 16, share))], axis=2)
        out_grad = lax.optimization_barrier(rows_by_rows(mixer, dbranch).astype(BF))
        out_grad = jnp.concatenate(
            [out_grad[:, i * LANES : (i + 1) * LANES].reshape(nb, ch, LANES) for i in range(slabs)], axis=1
        )
        kernel_grad = kernel_grad.astype(BF).reshape(taps, nb, ch).transpose(1, 0, 2).reshape(nb, taps * ch)
        kernel_grad = jnp.pad(kernel_grad, ((0, 0), (0, 16 * share - taps * ch))).reshape(nb, 16, share)
        in_grad, out_grad, kernel_grad = lax.optimization_barrier(
            (in_grad.reshape(nb, split, share), out_grad, kernel_grad)
        )
        conv_grad = after(jnp.concatenate([in_grad, out_grad, kernel_grad], axis=1), pair_sum)
        conv_grad = lax.psum_scatter(conv_grad, COLUMN, scatter_dimension=0)
        out_shard = conv_grad[split : split + slabs * ch].reshape(slabs, ch, LANES).transpose(1, 0, 2)
        out_shard = out_shard.reshape(ch, width).astype(F32)
        kernel_shard = conv_grad[split + slabs * ch :].reshape(-1)[: taps * ch].reshape(taps, ch).astype(F32)
        swapped = plane_swap(conv_grad[:split].reshape(4, 3 * r + 16, share), member)
        gain_shards = swapped[:, 3 * r :].reshape(4, 16 * share)[:, : 2 * r].astype(F32).sum(axis=0)
        place = jnp.arange(width).reshape(t, 2, 2, 2, ch).transpose(1, 3, 0, 2, 4).reshape(-1)
        order = (place[:, None] == jnp.arange(width)[None, :]).astype(BF)
        in_shard = swapped[:, : 3 * r].transpose(1, 0, 2).reshape(3 * r, width)
        in_shard = jnp.dot(in_shard, order, preferred_element_type=F32)
        in_shard = jnp.concatenate([in_shard[i * r : (i + 1) * r] for i in range(3)], axis=1)
        pair_shard = pair_shard.reshape(2, 2, r, 2, t, 2, h).transpose(3, 2, 4, 0, 5, 1, 6)
        pair_shard = pair_shard.reshape(2, r, 4 * nb * h).astype(F32)
        return (
            mixed,
            token_grad,
            gain_shards[:r],
            in_shard,
            kernel_shard,
            out_shard,
            gain_shards[r:],
            pair_shard[0],
            pair_shard[1],
            down_shard,
        )

    return local


def solution(mesh):
    t = mesh.shape["fsdp"] // 4
    grid = Mesh(mesh.devices.reshape(t, 2, 2, mesh.shape["rep"]), ("t", "b", "c", "y"))
    every = ("t", "b", "c", "y")
    in_specs = (
        P(every, None),
        P(every),
        P(every),
        P(every),
        P(every, None),
        P(None, every),
        P(every, None),
        P(every),
        P(every, None),
        P(every, None),
        P(every, None),
        P(every, None),
    )
    out_specs = (
        P(every, None),
        P(every, None),
        P(every),
        P(every, None),
        P(None, every),
        P(every, None),
        P(every),
        P(every, None),
        P(every, None),
        P(every, None),
    )
    return jax.shard_map(
        make_local(t), mesh=grid, in_specs=in_specs, out_specs=out_specs, check_vma=False
    )
```

```python
import jax
import jax.numpy as jnp
from jax import lax
from jax.sharding import Mesh, PartitionSpec as P

EPS = 1e-05
BF = jnp.bfloat16
F32 = jnp.float32

PLANE = ("b", "y")
COLUMN = ("t", "c")
LANES = 256


def rows_by_rows(left, right):
    return lax.dot_general(left, right, (((0,), (0,)), ((), ())), preferred_element_type=F32)


def cols_by_cols(left, right):
    return lax.dot_general(left, right, (((1,), (1,)), ((), ())), preferred_element_type=F32)


def to_peer(values, k):
    return lax.ppermute(values, PLANE, [(i, i ^ k) for i in range(4)])


def plane_gather(values):
    return [values] + [to_peer(values, k) for k in (1, 2, 3)]


def plane_sum(blocks, *others):
    sent = [after(blocks[k].astype(BF), *others) for k in (1, 2, 3)]
    total = blocks[0].astype(F32)
    for k in (1, 2, 3):
        total = total + to_peer(sent[k - 1], k).astype(F32)
    return total


def pick(blocks, i):
    return lax.dynamic_index_in_dim(blocks, i, 0, keepdims=False)


def plane_swap(blocks, member):
    got = [pick(blocks, member)] + [to_peer(pick(blocks, member ^ k), k) for k in (1, 2, 3)]
    got = jnp.stack(got)
    return jnp.stack([pick(got, member ^ j) for j in range(4)])


def after(values, *others):
    for other in others:
        if other.shape != values.shape:
            other = other[(slice(0, 1),) * other.ndim].reshape(())
        values = values + jnp.minimum(jnp.abs(other), 0).astype(values.dtype)
    return values


def tile_after(values, *others):
    corner = (0,) * values.ndim
    tile = lax.slice(values, corner, (1,) * (values.ndim - 2) + (16, 128))
    return lax.dynamic_update_slice(values, after(tile, *others), corner)


def norm_back(grad_norm, source, scale, gain):
    weighted = grad_norm * gain
    gain_grad = jnp.sum(grad_norm * source * scale, axis=0)
    row_mean = jnp.mean(weighted * source, axis=1, keepdims=True)
    source_grad = scale * weighted - source * scale**3 * row_mean
    return (source_grad, gain_grad, row_mean)


def shifted(values, steps):
    return jnp.pad(values, ((0, 0), (steps, 0), (0, 0)))[:, :-steps]


def lifted(values, steps):
    return jnp.pad(values, ((0, 0), (0, steps), (0, 0)))[:, steps:]


def make_local(t):
    nb = 2 * t

    def local(
        tokens,
        counts,
        segments,
        norm1_gain,
        in_weight,
        conv_kernel,
        out_weight,
        norm2_gain,
        gate_weight,
        up_weight,
        down_weight,
        cotangent,
    ):
        slots, width = tokens.shape
        r = in_weight.shape[0]
        ch = out_weight.shape[0]
        h = down_weight.shape[0]
        share = nb * ch
        taps = conv_kernel.shape[0]
        slabs = width // LANES
        member = 2 * lax.axis_index("b") + lax.axis_index("y")

        same_one = jnp.concatenate([jnp.zeros((1,), BF), (segments[1:] == segments[:-1]).astype(BF)])
        same_two = jnp.concatenate([jnp.zeros((2,), BF), (segments[2:] == segments[:-2]).astype(BF)])
        flags = jnp.concatenate([same_one, same_two])
        flags = jnp.pad(flags, (0, 16 * width - 2 * slots)).reshape(16, width)
        live = (jnp.arange(slots) < counts[0]).astype(F32)[:, None]
        dout = cotangent.astype(F32) * live
        dffn_own = dout.astype(BF)

        in_blocks = in_weight.reshape(r, 3, t, 2, 2, 2, ch).transpose(3, 5, 1, 0, 2, 4, 6)
        in_blocks = in_blocks.reshape(4, 3 * r, share)
        extra = jnp.concatenate([norm1_gain, norm2_gain, conv_kernel.reshape(-1)])
        extra = jnp.pad(extra, (0, 16 * share - extra.shape[0])).reshape(1, 16, share)
        conv_blocks = jnp.concatenate([in_blocks, jnp.broadcast_to(extra, (4, 16, share))], axis=1)
        conv_mine = plane_swap(conv_blocks, member)
        out_slabs = out_weight.reshape(ch, slabs, LANES).transpose(1, 0, 2).reshape(slabs * ch, LANES)
        conv_all = lax.all_gather(
            jnp.concatenate([conv_mine.reshape(4 * (3 * r + 16), share), out_slabs]), COLUMN
        )
        gathered = plane_gather(jnp.concatenate([tokens, flags]))
        source = jnp.stack([g[:slots] for g in gathered]).reshape(4 * slots, width).astype(F32)
        marks = jnp.stack([g[slots:].reshape(-1)[: 2 * slots] for g in gathered]).astype(F32)
        same_one = marks[:, :slots, None]
        same_two = marks[:, slots:, None]
        source, same_one, same_two = lax.optimization_barrier((source, same_one, same_two))

        def ff_blocks(w):
            return w.reshape(r, t, 2, 2, 2, h).transpose(2, 4, 0, 1, 3, 5).reshape(4, r, nb * h)

        tile = sum(g[:16, :128] for g in gathered[1:])
        pair = after(jnp.concatenate([ff_blocks(gate_weight), ff_blocks(up_weight)], axis=2), tile)
        pair_mine = plane_swap(pair, member).reshape(4 * r, 2 * nb * h)
        dffn = plane_gather(after(dffn_own, *[g[:slots] for g in gathered[1:]]))
        pair_all = lax.all_gather(pair_mine, COLUMN)
        pair_full = pair_all.reshape(t, 2, 2, 2 * r, 2 * nb * h).transpose(0, 2, 1, 3, 4)
        pair_full = lax.optimization_barrier(pair_full.reshape(width, 2 * nb * h))
        down_full = lax.all_gather(down_weight, COLUMN, axis=0, tiled=True)

        split = 4 * (3 * r + 16)
        head = conv_all[:, :split].reshape(t, 2, 2, 2, 3 * r + 16, share)
        in_full = head[:, :, :, :, : 3 * r].reshape(t, 2, 2, 2, 3, r, share)
        in_full = lax.optimization_barrier(
            in_full.transpose(0, 2, 1, 3, 5, 4, 6).reshape(width, 3 * share)
        )
        rest = head[:, :, :, :, 3 * r :].reshape(nb, 4, 16 * share)
        gains = rest[:, :, : 2 * r].reshape(t, 2, 2, 2, 2, r).transpose(4, 0, 2, 1, 3, 5)
        gains = gains.reshape(2, width).astype(F32)
        gains = lax.optimization_barrier(gains)
        gain_first, gain_second = gains[0], gains[1]
        kernel_vals = pick(rest.transpose(1, 0, 2), member)[:, 2 * r : 2 * r + taps * ch]
        kernel_vals = kernel_vals.reshape(nb, taps, ch).transpose(1, 0, 2).reshape(taps, share).astype(F32)
        out_full = conv_all[:, split:].reshape(nb, slabs, ch, LANES).transpose(0, 2, 1, 3)
        out_full, kernel_vals = lax.optimization_barrier((out_full.reshape(share, width), kernel_vals))

        scale_one = lax.rsqrt(jnp.mean(source * source, axis=1, keepdims=True) + EPS)
        normed_one = (source * scale_one * gain_first).astype(BF)
        projected = jnp.dot(normed_one, in_full, preferred_element_type=F32)
        projected = projected.reshape(4, slots, 3 * share)
        first = projected[:, :, :share]
        second = projected[:, :, share : 2 * share]
        stream = projected[:, :, 2 * share :]
        product = first * stream
        back_one = shifted(product, 1) * same_one
        back_two = shifted(product, 2) * same_two
        convolved = kernel_vals[0] * product + kernel_vals[1] * back_one + kernel_vals[2] * back_two
        mixer = (second * convolved).astype(BF).reshape(4 * slots, share)
        branch = jnp.dot(mixer, out_full, preferred_element_type=F32).reshape(4, slots, width)
        own = tokens.astype(F32)
        hidden = own + plane_sum(branch, *dffn[1:])
        dffn = jnp.concatenate(dffn)

        scale_two = lax.rsqrt(jnp.mean(hidden * hidden, axis=1, keepdims=True) + EPS)
        normed_two_own = (hidden * scale_two * gain_second).astype(BF)
        normed_two = plane_gather(normed_two_own)
        normed_two = jnp.concatenate(normed_two)
        both = jnp.dot(normed_two, pair_full, preferred_element_type=F32)
        gate = both[:, : nb * h]
        upper = both[:, nb * h :]
        sigma = jax.nn.sigmoid(gate)
        swish = gate * sigma
        act = (swish * upper).astype(BF)
        down_grad = rows_by_rows(act, dffn).astype(BF)
        down_sum = lax.psum_scatter(down_grad, COLUMN, scatter_dimension=0, tiled=True)
        down_shard = down_sum.astype(F32)
        dact = after(cols_by_cols(dffn, down_full), down_grad)
        dgate = (dact * upper * sigma * (1.0 + gate * (1.0 - sigma))).astype(BF)
        dupper = (dact * swish).astype(BF)
        dboth = jnp.concatenate([dgate, dupper], axis=1)
        dnormed_part = cols_by_cols(dboth, pair_full).reshape(4, slots, width)
        pair_grad = lax.optimization_barrier(rows_by_rows(normed_two, dboth).astype(BF))
        dnormed_two = plane_sum(dnormed_part)
        hidden_part, gain_two_grad, row_mean = norm_back(dnormed_two, hidden, scale_two, gain_second)
        pair_grad = pair_grad.reshape(t, 2, 2, 2 * r, 2 * nb * h).transpose(0, 2, 1, 3, 4)
        pair_grad = lax.optimization_barrier(pair_grad.reshape(nb, 4 * r, 2 * nb * h))
        pair_grad = tile_after(pair_grad, down_sum, row_mean)
        pair_sum = lax.psum_scatter(pair_grad, COLUMN, scatter_dimension=0)
        dhidden = dout + hidden_part

        dbranch = plane_gather(dhidden.astype(BF))
        dbranch_parts = dbranch[1:]
        dbranch = jnp.concatenate(dbranch)
        ffn = jnp.dot(act, down_full, preferred_element_type=F32).reshape(4, slots, width)
        ffn = plane_sum(lax.optimization_barrier(ffn), *dbranch_parts)
        mixed = (live * (hidden + ffn)).astype(BF)
        dmixer = cols_by_cols(dbranch, out_full).reshape(4, slots, share)
        dsecond = dmixer * convolved
        dconv = dmixer * second
        kernel_grad = jnp.stack(
            [
                jnp.sum(dconv * product, axis=(0, 1)),
                jnp.sum(dconv * back_one, axis=(0, 1)),
                jnp.sum(dconv * back_two, axis=(0, 1)),
            ]
        )
        dproduct = (
            kernel_vals[0] * dconv
            + kernel_vals[1] * lifted(dconv * same_one, 1)
            + kernel_vals[2] * lifted(dconv * same_two, 2)
        )
        dprojected = jnp.concatenate([dproduct * stream, dsecond, dproduct * first], axis=2)
        dprojected = after(dprojected.astype(BF).reshape(4 * slots, 3 * share), mixed[:16, :128])
        dnormed_part = cols_by_cols(dprojected, in_full)
        gain_one_grad = jnp.sum(dnormed_part * source * scale_one, axis=0)
        pair_shard = plane_swap(pair_sum.reshape(4, r, 2 * nb * h), member)
        dnormed_one = plane_sum(dnormed_part.reshape(4, slots, width), pair_shard[3])
        own_scale = scale_one[:slots]
        weighted = dnormed_one * gain_first
        token_grad = (
            dhidden
            + own_scale * weighted
            - own * own_scale**3 * jnp.mean(weighted * own, axis=1, keepdims=True)
        )

        kernel_grad, gain_one_grad, gain_two_grad = lax.optimization_barrier(
            (kernel_grad, gain_one_grad, gain_two_grad)
        )
        in_grad = lax.optimization_barrier(rows_by_rows(normed_one, dprojected).astype(BF))
        in_grad = jnp.stack(
            [
                in_grad[:, i * share : (i + 1) * share].reshape(t, 2, 2, 2, r, share).transpose(0, 2, 1, 3, 4, 5)
                for i in range(3)
            ],
            axis=4,
        )
        in_grad = in_grad.reshape(nb, 4, 3 * r, share)
        gain_grads = jnp.stack([gain_one_grad, gain_two_grad]).astype(BF)
        gain_grads = gain_grads.reshape(2, t, 2, 2, 2, r).transpose(1, 3, 2, 4, 0, 5).reshape(nb, 4, 2 * r)
        gain_grads = jnp.pad(gain_grads, ((0, 0), (0, 0), (0, 16 * share - 2 * r)))
        in_grad = jnp.concatenate([in_grad, lax.optimization_barrier(gain_grads.reshape(nb, 4, 16, share))], axis=2)
        out_grad = lax.optimization_barrier(rows_by_rows(mixer, dbranch).astype(BF))
        out_grad = jnp.concatenate(
            [out_grad[:, i * LANES : (i + 1) * LANES].reshape(nb, ch, LANES) for i in range(slabs)], axis=1
        )
        kernel_grad = kernel_grad.astype(BF).reshape(taps, nb, ch).transpose(1, 0, 2).reshape(nb, taps * ch)
        kernel_grad = jnp.pad(kernel_grad, ((0, 0), (0, 16 * share - taps * ch))).reshape(nb, 16, share)
        in_grad, out_grad, kernel_grad = lax.optimization_barrier(
            (in_grad.reshape(nb, split, share), out_grad, kernel_grad)
        )
        conv_grad = after(jnp.concatenate([in_grad, out_grad, kernel_grad], axis=1), pair_sum)
        conv_grad = lax.psum_scatter(conv_grad, COLUMN, scatter_dimension=0)
        out_shard = conv_grad[split : split + slabs * ch].reshape(slabs, ch, LANES).transpose(1, 0, 2)
        out_shard = out_shard.reshape(ch, width).astype(F32)
        kernel_shard = conv_grad[split + slabs * ch :].reshape(-1)[: taps * ch].reshape(taps, ch).astype(F32)
        swapped = plane_swap(conv_grad[:split].reshape(4, 3 * r + 16, share), member)
        gain_shards = swapped[:, 3 * r :].reshape(4, 16 * share)[:, : 2 * r].astype(F32).sum(axis=0)
        place = jnp.arange(width).reshape(t, 2, 2, 2, ch).transpose(1, 3, 0, 2, 4).reshape(-1)
        order = (place[:, None] == jnp.arange(width)[None, :]).astype(BF)
        in_shard = swapped[:, : 3 * r].transpose(1, 0, 2).reshape(3 * r, width)
        in_shard = jnp.dot(in_shard, order, preferred_element_type=F32)
        in_shard = jnp.concatenate([in_shard[i * r : (i + 1) * r] for i in range(3)], axis=1)
        pair_shard = pair_shard.reshape(2, 2, r, 2, t, 2, h).transpose(3, 2, 4, 0, 5, 1, 6)
        pair_shard = pair_shard.reshape(2, r, 4 * nb * h).astype(F32)
        return (
            mixed,
            token_grad,
            gain_shards[:r],
            in_shard,
            kernel_shard,
            out_shard,
            gain_shards[r:],
            pair_shard[0],
            pair_shard[1],
            down_shard,
        )

    return local


def solution(mesh):
    t = mesh.shape["fsdp"] // 4
    grid = Mesh(mesh.devices.reshape(t, 2, 2, mesh.shape["rep"]), ("t", "b", "c", "y"))
    every = ("t", "b", "c", "y")
    in_specs = (
        P(every, None),
        P(every),
        P(every),
        P(every),
        P(every, None),
        P(None, every),
        P(every, None),
        P(every),
        P(every, None),
        P(every, None),
        P(every, None),
        P(every, None),
    )
    out_specs = (
        P(every, None),
        P(every, None),
        P(every),
        P(every, None),
        P(None, every),
        P(every, None),
        P(every),
        P(every, None),
        P(every, None),
        P(every, None),
    )
    return jax.shard_map(
        make_local(t), mesh=grid, in_specs=in_specs, out_specs=out_specs, check_vma=False
    )
```

```python
import jax
import jax.numpy as jnp
from jax import lax
from jax.sharding import Mesh, PartitionSpec as P

EPS = 1e-05
BF = jnp.bfloat16
F32 = jnp.float32

PLANE = ("b", "y")
COLUMN = ("t", "c")
LANES = 256


def rows_by_rows(left, right):
    return lax.dot_general(left, right, (((0,), (0,)), ((), ())), preferred_element_type=F32)


def cols_by_cols(left, right):
    return lax.dot_general(left, right, (((1,), (1,)), ((), ())), preferred_element_type=F32)


def to_peer(values, k):
    return lax.ppermute(values, PLANE, [(i, i ^ k) for i in range(4)])


def plane_gather(values):
    return [values] + [to_peer(values, k) for k in (1, 2, 3)]


def plane_sum(blocks, *others):
    sent = [after(blocks[k].astype(BF), *others) for k in (1, 2, 3)]
    total = blocks[0].astype(F32)
    for k in (1, 2, 3):
        total = total + to_peer(sent[k - 1], k).astype(F32)
    return total


def pick(blocks, i):
    return lax.dynamic_index_in_dim(blocks, i, 0, keepdims=False)


def plane_swap(blocks, member):
    got = [pick(blocks, member)] + [to_peer(pick(blocks, member ^ k), k) for k in (1, 2, 3)]
    got = jnp.stack(got)
    return jnp.stack([pick(got, member ^ j) for j in range(4)])


def after(values, *others):
    for other in others:
        if other.shape != values.shape:
            other = other[(slice(0, 1),) * other.ndim].reshape(())
        values = values + jnp.minimum(jnp.abs(other), 0).astype(values.dtype)
    return values


def tile_after(values, *others):
    corner = (0,) * values.ndim
    tile = lax.slice(values, corner, (1,) * (values.ndim - 2) + (16, 128))
    return lax.dynamic_update_slice(values, after(tile, *others), corner)


def norm_back(grad_norm, source, scale, gain):
    weighted = grad_norm * gain
    gain_grad = jnp.sum(grad_norm * source * scale, axis=0)
    row_mean = jnp.mean(weighted * source, axis=1, keepdims=True)
    source_grad = scale * weighted - source * scale**3 * row_mean
    return (source_grad, gain_grad, row_mean)


def shifted(values, steps):
    return jnp.pad(values, ((0, 0), (steps, 0), (0, 0)))[:, :-steps]


def lifted(values, steps):
    return jnp.pad(values, ((0, 0), (0, steps), (0, 0)))[:, steps:]


def make_local(t):
    nb = 2 * t

    def local(
        tokens,
        counts,
        segments,
        norm1_gain,
        in_weight,
        conv_kernel,
        out_weight,
        norm2_gain,
        gate_weight,
        up_weight,
        down_weight,
        cotangent,
    ):
        slots, width = tokens.shape
        r = in_weight.shape[0]
        ch = out_weight.shape[0]
        h = down_weight.shape[0]
        share = nb * ch
        taps = conv_kernel.shape[0]
        slabs = width // LANES
        member = 2 * lax.axis_index("b") + lax.axis_index("y")

        same_one = jnp.concatenate([jnp.zeros((1,), BF), (segments[1:] == segments[:-1]).astype(BF)])
        same_two = jnp.concatenate([jnp.zeros((2,), BF), (segments[2:] == segments[:-2]).astype(BF)])
        live = (jnp.arange(slots) < counts[0]).astype(F32)[:, None]
        dout = cotangent.astype(F32) * live
        dffn_own = dout.astype(BF)

        in_blocks = in_weight.reshape(r, 3, t, 2, 2, 2, ch).transpose(3, 5, 1, 0, 2, 4, 6)
        in_blocks = in_blocks.reshape(4, 3 * r, share)
        extra = jnp.concatenate([norm1_gain, norm2_gain, conv_kernel.reshape(-1)])
        rows = 2 * slots // share
        extra = jnp.pad(extra, (0, share - extra.shape[0]))
        extra = jnp.concatenate([extra, same_one, same_two])
        extra = jnp.pad(extra, (0, 16 * share - extra.shape[0])).reshape(1, 16, share)
        conv_blocks = jnp.concatenate([in_blocks, jnp.broadcast_to(extra, (4, 16, share))], axis=1)
        conv_mine = plane_swap(conv_blocks, member)
        out_slabs = out_weight.reshape(ch, slabs, LANES).transpose(1, 0, 2).reshape(slabs * ch, LANES)
        conv_all = lax.all_gather(
            jnp.concatenate([conv_mine.reshape(4 * (3 * r + 16), share), out_slabs]), COLUMN
        )
        gathered = plane_gather(tokens)
        source = jnp.stack(gathered).reshape(4 * slots, width)
        marks = conv_mine[:, 3 * r + 1 : 3 * r + 1 + rows].reshape(4, 2 * slots)
        marks = jnp.stack([pick(marks, member ^ k) for k in range(4)]).astype(F32)
        same_one = marks[:, :slots, None]
        same_two = marks[:, slots:, None]
        source, same_one, same_two = lax.optimization_barrier((source, same_one, same_two))
        source = source.astype(F32)

        def ff_blocks(w):
            return w.reshape(r, t, 2, 2, 2, h).transpose(2, 4, 0, 1, 3, 5).reshape(4, r, nb * h)

        tile = sum(g[:16, :128] for g in gathered[1:])
        pair = after(jnp.concatenate([ff_blocks(gate_weight), ff_blocks(up_weight)], axis=2), tile)
        pair_mine = plane_swap(pair, member).reshape(4 * r, 2 * nb * h)
        dffn = plane_gather(after(dffn_own, *gathered[1:]))
        pair_all = lax.all_gather(pair_mine, COLUMN)
        pair_full = pair_all.reshape(t, 2, 2, 2 * r, 2 * nb * h).transpose(0, 2, 1, 3, 4)
        pair_full = lax.optimization_barrier(pair_full.reshape(width, 2 * nb * h))
        down_full = lax.all_gather(down_weight, COLUMN, axis=0, tiled=True)

        split = 4 * (3 * r + 16)
        head = conv_all[:, :split].reshape(t, 2, 2, 2, 3 * r + 16, share)
        in_parts = [
            head[:, :, :, :, i * r : (i + 1) * r].transpose(0, 2, 1, 3, 4, 5).reshape(width, share) for i in range(3)
        ]
        in_parts = lax.optimization_barrier(in_parts)
        rest = head[:, :, :, :, 3 * r].reshape(nb, 4, share)
        gains = rest[:, :, : 2 * r].reshape(t, 2, 2, 2, 2, r).transpose(4, 0, 2, 1, 3, 5)
        gains = gains.reshape(2, width).astype(F32)
        gains = lax.optimization_barrier(gains)
        gain_first, gain_second = gains[0], gains[1]
        kernel_vals = pick(rest.transpose(1, 0, 2), member)[:, 2 * r : 2 * r + taps * ch]
        kernel_vals = kernel_vals.reshape(nb, taps, ch).transpose(1, 0, 2).reshape(taps, share).astype(F32)
        out_full = conv_all[:, split:].reshape(nb, slabs, ch, LANES).transpose(0, 2, 1, 3)
        out_full, kernel_vals = lax.optimization_barrier((out_full.reshape(share, width), kernel_vals))

        scale_one = lax.rsqrt(jnp.mean(source * source, axis=1, keepdims=True) + EPS)
        normed_one = (source * scale_one * gain_first).astype(BF)
        first, second, stream = [
            jnp.dot(normed_one, part, preferred_element_type=F32).reshape(4, slots, share) for part in in_parts
        ]
        in_full = jnp.concatenate(in_parts, axis=1)
        product = first * stream
        back_one = shifted(product, 1) * same_one
        back_two = shifted(product, 2) * same_two
        convolved = kernel_vals[0] * product + kernel_vals[1] * back_one + kernel_vals[2] * back_two
        mixer = (second * convolved).astype(BF).reshape(4 * slots, share)
        branch = jnp.dot(mixer, out_full, preferred_element_type=F32).reshape(4, slots, width)
        own = tokens.astype(F32)
        hidden = own + plane_sum(branch, *dffn[1:])
        dffn = jnp.concatenate(dffn)

        scale_two = lax.rsqrt(jnp.mean(hidden * hidden, axis=1, keepdims=True) + EPS)
        normed_two_own = (hidden * scale_two * gain_second).astype(BF)
        normed_two = plane_gather(normed_two_own)
        normed_two = jnp.concatenate(normed_two)
        gate = jnp.dot(normed_two, pair_full[:, : nb * h], preferred_element_type=F32)
        upper = jnp.dot(normed_two, pair_full[:, nb * h :], preferred_element_type=F32)
        sigma = jax.nn.sigmoid(gate)
        swish = gate * sigma
        act = (swish * upper).astype(BF)
        down_grad = rows_by_rows(act, dffn).astype(BF)
        down_sum = lax.psum_scatter(down_grad, COLUMN, scatter_dimension=0, tiled=True)
        down_shard = down_sum.astype(F32)
        dact = after(cols_by_cols(dffn, down_full), down_grad)
        dgate = (dact * upper * sigma * (1.0 + gate * (1.0 - sigma))).astype(BF)
        dupper = (dact * swish).astype(BF)
        dboth = jnp.concatenate([dgate, dupper], axis=1)
        dnormed_part = cols_by_cols(dboth, pair_full).reshape(4, slots, width)
        pair_grad = lax.optimization_barrier(rows_by_rows(normed_two, dboth).astype(BF))
        dnormed_two = plane_sum(dnormed_part)
        hidden_part, gain_two_grad, row_mean = norm_back(dnormed_two, hidden, scale_two, gain_second)
        pair_grad = pair_grad.reshape(t, 2, 2, 2 * r, 2 * nb * h).transpose(0, 2, 1, 3, 4)
        pair_grad = lax.optimization_barrier(pair_grad.reshape(nb, 4 * r, 2 * nb * h))
        pair_grad = tile_after(pair_grad, down_sum, row_mean)
        pair_sum = lax.psum_scatter(pair_grad, COLUMN, scatter_dimension=0)
        dhidden = dout + hidden_part

        dbranch = plane_gather(dhidden.astype(BF))
        dbranch_parts = dbranch[1:]
        dbranch = jnp.concatenate(dbranch)
        ffn = jnp.dot(act, down_full, preferred_element_type=F32).reshape(4, slots, width)
        ffn = plane_sum(lax.optimization_barrier(ffn), *dbranch_parts)
        mixed = (live * (hidden + ffn)).astype(BF)
        dmixer = cols_by_cols(dbranch, out_full).reshape(4, slots, share)
        dsecond = dmixer * convolved
        dconv = dmixer * second
        kernel_grad = jnp.stack(
            [
                jnp.sum(dconv * product, axis=(0, 1)),
                jnp.sum(dconv * back_one, axis=(0, 1)),
                jnp.sum(dconv * back_two, axis=(0, 1)),
            ]
        )
        dproduct = (
            kernel_vals[0] * dconv
            + kernel_vals[1] * lifted(dconv * same_one, 1)
            + kernel_vals[2] * lifted(dconv * same_two, 2)
        )
        dprojected = jnp.concatenate([dproduct * stream, dsecond, dproduct * first], axis=2)
        dprojected = dprojected.astype(BF).reshape(4 * slots, 3 * share)
        dnormed_part = cols_by_cols(dprojected, in_full)
        gain_one_grad = jnp.sum(dnormed_part * source * scale_one, axis=0)
        pair_shard = plane_swap(pair_sum.reshape(4, r, 2 * nb * h), member)
        dnormed_one = plane_sum(dnormed_part.reshape(4, slots, width), pair_shard[3])
        own_scale = scale_one[:slots]
        weighted = dnormed_one * gain_first
        token_grad = (
            dhidden
            + own_scale * weighted
            - own * own_scale**3 * jnp.mean(weighted * own, axis=1, keepdims=True)
        )

        kernel_grad, gain_one_grad, gain_two_grad = lax.optimization_barrier(
            (kernel_grad, gain_one_grad, gain_two_grad)
        )
        in_grad = after(rows_by_rows(normed_one, dprojected), mixed[:16, :128])
        in_grad = lax.optimization_barrier(in_grad.astype(BF))
        in_grad = jnp.stack(
            [
                in_grad[:, i * share : (i + 1) * share].reshape(t, 2, 2, 2, r, share).transpose(0, 2, 1, 3, 4, 5)
                for i in range(3)
            ],
            axis=4,
        )
        in_grad = in_grad.reshape(nb, 4, 3 * r, share)
        gain_grads = jnp.stack([gain_one_grad, gain_two_grad]).astype(BF)
        gain_grads = gain_grads.reshape(2, t, 2, 2, 2, r).transpose(1, 3, 2, 4, 0, 5).reshape(nb, 4, 2 * r)
        gain_grads = jnp.pad(gain_grads, ((0, 0), (0, 0), (0, 16 * share - 2 * r)))
        in_grad = jnp.concatenate([in_grad, lax.optimization_barrier(gain_grads.reshape(nb, 4, 16, share))], axis=2)
        out_grad = lax.optimization_barrier(rows_by_rows(mixer, dbranch).astype(BF))
        out_grad = jnp.concatenate(
            [out_grad[:, i * LANES : (i + 1) * LANES].reshape(nb, ch, LANES) for i in range(slabs)], axis=1
        )
        kernel_grad = kernel_grad.astype(BF).reshape(taps, nb, ch).transpose(1, 0, 2).reshape(nb, taps * ch)
        kernel_grad = jnp.pad(kernel_grad, ((0, 0), (0, 16 * share - taps * ch))).reshape(nb, 16, share)
        in_grad, out_grad, kernel_grad = lax.optimization_barrier(
            (in_grad.reshape(nb, split, share), out_grad, kernel_grad)
        )
        conv_grad = after(jnp.concatenate([in_grad, out_grad, kernel_grad], axis=1), pair_sum)
        conv_grad = lax.psum_scatter(conv_grad, COLUMN, scatter_dimension=0)
        out_shard = conv_grad[split : split + slabs * ch].reshape(slabs, ch, LANES).transpose(1, 0, 2)
        out_shard = out_shard.reshape(ch, width).astype(F32)
        kernel_shard = conv_grad[split + slabs * ch, : taps * ch].reshape(taps, ch).astype(F32)
        parts = conv_grad[:split].reshape(4, 3 * r + 16, share)
        parts = [pick(parts, member)] + [to_peer(pick(parts, member ^ k), k) for k in (1, 2, 3)]
        gain_shards = sum(p[3 * r, : 2 * r].astype(F32) for p in parts)
        place = jnp.arange(width).reshape(t, 2, 2, 2, ch).transpose(1, 3, 0, 2, 4).reshape(4, share)
        place = jnp.concatenate([pick(place, member ^ k) for k in range(4)])
        order = (place[:, None] == jnp.arange(width)[None, :]).astype(BF)
        in_shard = jnp.concatenate([p[: 3 * r] for p in parts], axis=1)
        in_shard = jnp.dot(in_shard, order, preferred_element_type=F32)
        in_shard = jnp.concatenate([in_shard[i * r : (i + 1) * r] for i in range(3)], axis=1)
        pair_shard = pair_shard.reshape(2, 2, r, 2, t, 2, h).transpose(3, 2, 4, 0, 5, 1, 6)
        pair_shard = pair_shard.reshape(2, r, 4 * nb * h).astype(F32)
        return (
            mixed,
            token_grad,
            gain_shards[:r],
            in_shard,
            kernel_shard,
            out_shard,
            gain_shards[r:],
            pair_shard[0],
            pair_shard[1],
            down_shard,
        )

    return local


def solution(mesh):
    t = mesh.shape["fsdp"] // 4
    grid = Mesh(mesh.devices.reshape(t, 2, 2, mesh.shape["rep"]), ("t", "b", "c", "y"))
    every = ("t", "b", "c", "y")
    in_specs = (
        P(every, None),
        P(every),
        P(every),
        P(every),
        P(every, None),
        P(None, every),
        P(every, None),
        P(every),
        P(every, None),
        P(every, None),
        P(every, None),
        P(every, None),
    )
    out_specs = (
        P(every, None),
        P(every, None),
        P(every),
        P(every, None),
        P(None, every),
        P(every, None),
        P(every),
        P(every, None),
        P(every, None),
        P(every, None),
    )
    return jax.shard_map(
        make_local(t), mesh=grid, in_specs=in_specs, out_specs=out_specs, check_vma=False
    )
```

```python
import jax
import jax.numpy as jnp
from jax import lax
from jax.sharding import Mesh, PartitionSpec as P

EPS = 1e-05
BF = jnp.bfloat16
F32 = jnp.float32

PLANE = ("b", "y")
COLUMN = ("t", "c")
LANES = 256


def rows_by_rows(left, right):
    return lax.dot_general(left, right, (((0,), (0,)), ((), ())), preferred_element_type=F32)


def cols_by_cols(left, right):
    return lax.dot_general(left, right, (((1,), (1,)), ((), ())), preferred_element_type=F32)


def to_peer(values, k):
    return lax.ppermute(values, PLANE, [(i, i ^ k) for i in range(4)])


def plane_gather(values):
    return [values] + [to_peer(values, k) for k in (1, 2, 3)]


def plane_sum(blocks, *others):
    sent = [after(blocks[k].astype(BF), *others) for k in (1, 2, 3)]
    total = blocks[0].astype(F32)
    for k in (1, 2, 3):
        total = total + to_peer(sent[k - 1], k).astype(F32)
    return total


def pick(blocks, i):
    return lax.dynamic_index_in_dim(blocks, i, 0, keepdims=False)


def plane_swap(blocks, member):
    got = [pick(blocks, member)] + [to_peer(pick(blocks, member ^ k), k) for k in (1, 2, 3)]
    got = jnp.stack(got)
    return jnp.stack([pick(got, member ^ j) for j in range(4)])


def after(values, *others):
    for other in others:
        if other.shape != values.shape:
            other = other[(slice(0, 1),) * other.ndim].reshape(())
        values = values + jnp.minimum(jnp.abs(other), 0).astype(values.dtype)
    return values


def tile_after(values, *others):
    corner = (0,) * values.ndim
    tile = lax.slice(values, corner, (1,) * (values.ndim - 2) + (16, 128))
    return lax.dynamic_update_slice(values, after(tile, *others), corner)


def norm_back(grad_norm, source, scale, gain):
    weighted = grad_norm * gain
    gain_grad = jnp.sum(grad_norm * source * scale, axis=0)
    row_mean = jnp.mean(weighted * source, axis=1, keepdims=True)
    source_grad = scale * weighted - source * scale**3 * row_mean
    return (source_grad, gain_grad, row_mean)


def shifted(values, steps):
    return jnp.pad(values, ((0, 0), (steps, 0), (0, 0)))[:, :-steps]


def lifted(values, steps):
    return jnp.pad(values, ((0, 0), (0, steps), (0, 0)))[:, steps:]


def make_local(t):
    nb = 2 * t

    def local(
        tokens,
        counts,
        segments,
        norm1_gain,
        in_weight,
        conv_kernel,
        out_weight,
        norm2_gain,
        gate_weight,
        up_weight,
        down_weight,
        cotangent,
    ):
        slots, width = tokens.shape
        r = in_weight.shape[0]
        ch = out_weight.shape[0]
        h = down_weight.shape[0]
        share = nb * ch
        taps = conv_kernel.shape[0]
        slabs = width // LANES
        member = 2 * lax.axis_index("b") + lax.axis_index("y")

        same_one = jnp.concatenate([jnp.zeros((1,), BF), (segments[1:] == segments[:-1]).astype(BF)])
        same_two = jnp.concatenate([jnp.zeros((2,), BF), (segments[2:] == segments[:-2]).astype(BF)])
        live = (jnp.arange(slots) < counts[0]).astype(F32)[:, None]
        dout = cotangent.astype(F32) * live
        dffn_own = dout.astype(BF)

        in_blocks = in_weight.reshape(r, 3, t, 2, 2, 2, ch).transpose(3, 5, 1, 0, 2, 4, 6)
        in_blocks = in_blocks.reshape(4, 3 * r, share)
        extra = jnp.concatenate([norm1_gain, norm2_gain, conv_kernel.reshape(-1)])
        rows = 2 * slots // share
        extra = jnp.pad(extra, (0, share - extra.shape[0]))
        extra = jnp.concatenate([extra, same_one, same_two])
        extra = jnp.pad(extra, (0, 16 * share - extra.shape[0])).reshape(1, 16, share)
        conv_blocks = jnp.concatenate([in_blocks, jnp.broadcast_to(extra, (4, 16, share))], axis=1)
        conv_mine = plane_swap(conv_blocks, member)
        out_slabs = out_weight.reshape(ch, slabs, LANES).transpose(1, 0, 2).reshape(slabs * ch, LANES)
        conv_all = lax.all_gather(
            jnp.concatenate([conv_mine.reshape(4 * (3 * r + 16), share), out_slabs]), COLUMN
        )
        gathered = plane_gather(tokens)
        source = jnp.stack(gathered).reshape(4 * slots, width)
        marks = conv_mine[:, 3 * r + 1 : 3 * r + 1 + rows].reshape(4, 2 * slots)
        marks = jnp.stack([pick(marks, member ^ k) for k in range(4)]).astype(F32)
        same_one = marks[:, :slots, None]
        same_two = marks[:, slots:, None]
        source, same_one, same_two = lax.optimization_barrier((source, same_one, same_two))
        source = source.astype(F32)

        def ff_blocks(w):
            return w.reshape(r, t, 2, 2, 2, h).transpose(2, 4, 0, 1, 3, 5).reshape(4, r, nb * h)

        tile = sum(g[:16, :128] for g in gathered[1:])
        pair = after(jnp.concatenate([ff_blocks(gate_weight), ff_blocks(up_weight)], axis=2), tile)
        pair_mine = plane_swap(pair, member).reshape(4 * r, 2 * nb * h)
        dffn = plane_gather(after(dffn_own, *gathered[1:]))
        pair_all = lax.all_gather(pair_mine, COLUMN)
        pair_full = pair_all.reshape(t, 2, 2, 2 * r, 2 * nb * h).transpose(0, 2, 1, 3, 4)
        pair_full = lax.optimization_barrier(pair_full.reshape(width, 2 * nb * h))
        down_full = lax.all_gather(down_weight, COLUMN, axis=0, tiled=True)

        split = 4 * (3 * r + 16)
        head = conv_all[:, :split].reshape(t, 2, 2, 2, 3 * r + 16, share)
        in_parts = [
            head[:, :, :, :, i * r : (i + 1) * r].transpose(0, 2, 1, 3, 4, 5).reshape(width, share) for i in range(3)
        ]
        in_parts = lax.optimization_barrier(in_parts)
        rest = head[:, :, :, :, 3 * r].reshape(nb, 4, share)
        gains = rest[:, :, : 2 * r].reshape(t, 2, 2, 2, 2, r).transpose(4, 0, 2, 1, 3, 5)
        gains = gains.reshape(2, width).astype(F32)
        gains = lax.optimization_barrier(gains)
        gain_first, gain_second = gains[0], gains[1]
        kernel_vals = pick(rest.transpose(1, 0, 2), member)[:, 2 * r : 2 * r + taps * ch]
        kernel_vals = kernel_vals.reshape(nb, taps, ch).transpose(1, 0, 2).reshape(taps, share).astype(F32)
        out_full = conv_all[:, split:].reshape(nb, slabs, ch, LANES).transpose(0, 2, 1, 3)
        out_full, kernel_vals = lax.optimization_barrier((out_full.reshape(share, width), kernel_vals))

        scale_one = lax.rsqrt(jnp.mean(source * source, axis=1, keepdims=True) + EPS)
        normed_one = (source * scale_one * gain_first).astype(BF)
        first, second, stream = [
            jnp.dot(normed_one, part, preferred_element_type=F32).reshape(4, slots, share) for part in in_parts
        ]
        in_full = jnp.concatenate(in_parts, axis=1)
        product = first * stream
        back_one = shifted(product, 1) * same_one
        back_two = shifted(product, 2) * same_two
        convolved = kernel_vals[0] * product + kernel_vals[1] * back_one + kernel_vals[2] * back_two
        mixer = (second * convolved).astype(BF).reshape(4 * slots, share)
        branch = jnp.dot(mixer, out_full, preferred_element_type=F32).reshape(4, slots, width)
        own = tokens.astype(F32)
        hidden = own + plane_sum(branch, *dffn[1:])
        dffn = lax.optimization_barrier(jnp.concatenate(dffn))

        scale_two = lax.rsqrt(jnp.mean(hidden * hidden, axis=1, keepdims=True) + EPS)
        normed_two_own = (hidden * scale_two * gain_second).astype(BF)
        normed_two = plane_gather(normed_two_own)
        normed_two = jnp.concatenate(normed_two)
        gate = jnp.dot(normed_two, pair_full[:, : nb * h], preferred_element_type=F32)
        upper = jnp.dot(normed_two, pair_full[:, nb * h :], preferred_element_type=F32)
        sigma = jax.nn.sigmoid(gate)
        swish = gate * sigma
        act = (swish * upper).astype(BF)
        down_grad = rows_by_rows(act, dffn).astype(BF)
        down_sum = lax.psum_scatter(down_grad, COLUMN, scatter_dimension=0, tiled=True)
        down_shard = down_sum.astype(F32)
        dact = after(cols_by_cols(dffn, down_full), down_grad)
        dgate = (dact * upper * sigma * (1.0 + gate * (1.0 - sigma))).astype(BF)
        dupper = (dact * swish).astype(BF)
        dboth = jnp.concatenate([dgate, dupper], axis=1)
        dnormed_part = cols_by_cols(dboth, pair_full).reshape(4, slots, width)
        pair_grad = lax.optimization_barrier(rows_by_rows(normed_two, dboth).astype(BF))
        dnormed_two = plane_sum(dnormed_part)
        hidden_part, gain_two_grad, row_mean = norm_back(dnormed_two, hidden, scale_two, gain_second)
        pair_grad = pair_grad.reshape(t, 2, 2, 2 * r, 2 * nb * h).transpose(0, 2, 1, 3, 4)
        pair_grad = lax.optimization_barrier(pair_grad.reshape(nb, 4 * r, 2 * nb * h))
        pair_grad = tile_after(pair_grad, down_sum, row_mean)
        pair_sum = lax.psum_scatter(pair_grad, COLUMN, scatter_dimension=0)
        dhidden = dout + hidden_part

        dbranch = plane_gather(dhidden.astype(BF))
        dbranch_parts = dbranch[1:]
        dbranch = jnp.concatenate(dbranch)
        ffn = jnp.dot(act, down_full, preferred_element_type=F32).reshape(4, slots, width)
        ffn = plane_sum(lax.optimization_barrier(ffn), *dbranch_parts)
        mixed = (live * (hidden + ffn)).astype(BF)
        dmixer = cols_by_cols(dbranch, out_full).reshape(4, slots, share)
        dsecond = dmixer * convolved
        dconv = dmixer * second
        kernel_grad = jnp.stack(
            [
                jnp.sum(dconv * product, axis=(0, 1)),
                jnp.sum(dconv * back_one, axis=(0, 1)),
                jnp.sum(dconv * back_two, axis=(0, 1)),
            ]
        )
        dproduct = (
            kernel_vals[0] * dconv
            + kernel_vals[1] * lifted(dconv * same_one, 1)
            + kernel_vals[2] * lifted(dconv * same_two, 2)
        )
        dprojected = jnp.concatenate([dproduct * stream, dsecond, dproduct * first], axis=2)
        dprojected = dprojected.astype(BF).reshape(4 * slots, 3 * share)
        dnormed_part = cols_by_cols(dprojected, in_full)
        gain_one_grad = jnp.sum(dnormed_part * source * scale_one, axis=0)
        pair_shard = plane_swap(pair_sum.reshape(4, r, 2 * nb * h), member)
        dnormed_one = plane_sum(dnormed_part.reshape(4, slots, width), pair_shard[3])
        own_scale = scale_one[:slots]
        weighted = dnormed_one * gain_first
        token_grad = (
            dhidden
            + own_scale * weighted
            - own * own_scale**3 * jnp.mean(weighted * own, axis=1, keepdims=True)
        )

        kernel_grad, gain_one_grad, gain_two_grad = lax.optimization_barrier(
            (kernel_grad, gain_one_grad, gain_two_grad)
        )
        in_grad = after(rows_by_rows(normed_one, dprojected), mixed[:16, :128])
        in_grad = lax.optimization_barrier(in_grad.astype(BF))
        in_grad = jnp.stack(
            [
                in_grad[:, i * share : (i + 1) * share].reshape(t, 2, 2, 2, r, share).transpose(0, 2, 1, 3, 4, 5)
                for i in range(3)
            ],
            axis=4,
        )
        in_grad = in_grad.reshape(nb, 4, 3 * r, share)
        gain_grads = jnp.stack([gain_one_grad, gain_two_grad]).astype(BF)
        gain_grads = gain_grads.reshape(2, t, 2, 2, 2, r).transpose(1, 3, 2, 4, 0, 5).reshape(nb, 4, 2 * r)
        gain_grads = jnp.pad(gain_grads, ((0, 0), (0, 0), (0, 16 * share - 2 * r)))
        in_grad = jnp.concatenate([in_grad, lax.optimization_barrier(gain_grads.reshape(nb, 4, 16, share))], axis=2)
        out_grad = lax.optimization_barrier(rows_by_rows(mixer, dbranch).astype(BF))
        out_grad = jnp.concatenate(
            [out_grad[:, i * LANES : (i + 1) * LANES].reshape(nb, ch, LANES) for i in range(slabs)], axis=1
        )
        kernel_grad = kernel_grad.astype(BF).reshape(taps, nb, ch).transpose(1, 0, 2).reshape(nb, taps * ch)
        kernel_grad = jnp.pad(kernel_grad, ((0, 0), (0, 16 * share - taps * ch))).reshape(nb, 16, share)
        in_grad, out_grad, kernel_grad = lax.optimization_barrier(
            (in_grad.reshape(nb, split, share), out_grad, kernel_grad)
        )
        conv_grad = after(jnp.concatenate([in_grad, out_grad, kernel_grad], axis=1), pair_sum)
        conv_grad = lax.psum_scatter(conv_grad, COLUMN, scatter_dimension=0)
        out_shard = conv_grad[split : split + slabs * ch].reshape(slabs, ch, LANES).transpose(1, 0, 2)
        out_shard = out_shard.reshape(ch, width).astype(F32)
        kernel_shard = conv_grad[split + slabs * ch, : taps * ch].reshape(taps, ch).astype(F32)
        parts = conv_grad[:split].reshape(4, 3 * r + 16, share)
        parts = [pick(parts, member)] + [to_peer(pick(parts, member ^ k), k) for k in (1, 2, 3)]
        gain_shards = sum(p[3 * r, : 2 * r].astype(F32) for p in parts)
        place = jnp.arange(width).reshape(t, 2, 2, 2, ch).transpose(1, 3, 0, 2, 4).reshape(4, share)
        place = jnp.concatenate([pick(place, member ^ k) for k in range(4)])
        order = (place[:, None] == jnp.arange(width)[None, :]).astype(BF)
        in_shard = jnp.concatenate([p[: 3 * r] for p in parts], axis=1)
        in_shard = jnp.dot(in_shard, order, preferred_element_type=F32)
        in_shard = jnp.concatenate([in_shard[i * r : (i + 1) * r] for i in range(3)], axis=1)
        pair_shard = pair_shard.reshape(2, 2, r, 2, t, 2, h).transpose(3, 2, 4, 0, 5, 1, 6)
        pair_shard = pair_shard.reshape(2, r, 4 * nb * h).astype(F32)
        return (
            mixed,
            token_grad,
            gain_shards[:r],
            in_shard,
            kernel_shard,
            out_shard,
            gain_shards[r:],
            pair_shard[0],
            pair_shard[1],
            down_shard,
        )

    return local


def solution(mesh):
    t = mesh.shape["fsdp"] // 4
    grid = Mesh(mesh.devices.reshape(t, 2, 2, mesh.shape["rep"]), ("t", "b", "c", "y"))
    every = ("t", "b", "c", "y")
    in_specs = (
        P(every, None),
        P(every),
        P(every),
        P(every),
        P(every, None),
        P(None, every),
        P(every, None),
        P(every),
        P(every, None),
        P(every, None),
        P(every, None),
        P(every, None),
    )
    out_specs = (
        P(every, None),
        P(every, None),
        P(every),
        P(every, None),
        P(None, every),
        P(every, None),
        P(every),
        P(every, None),
        P(every, None),
        P(every, None),
    )
    return jax.shard_map(
        make_local(t), mesh=grid, in_specs=in_specs, out_specs=out_specs, check_vma=False
    )
```
